32 devices in a mesh: row: 4 (over y, core), col: 8 (over z, x).
Axes of the slice: x: 2, y: 2, z: 4, core: 2. Of those that a mesh axis runs over, the one named last changes fastest.
Arguments:
- matrix: float32 [4, 4, 256, 2, 8, 256], P(None, 'row', None, None, 'col'), as said below
- vectors: float32 [4, 4, 256, 256], P(None, 'row'), may hold values from -0.09375 to 0.09375
- t_factor: float32 [256, 256], replicated, as said below
Outputs:
- updated: float32 [4, 4, 256, 2, 8, 256], P(None, 'row', None, None, 'col')
The draws below stay inside these ranges and needn't reach their ends.
Inputs may be any that keep to these rules, and one draw needn't show every extreme that they name: matrix is exactly symmetric as an 4096 x 4096 matrix: entry (i, j) equals entry (j, i). t_factor is upper triangular with its diagonal between 0.5 and 1.5.
All inputs are finite; a program needn't handle non-finite values.
Results may differ from the reference program's by a relative error of at most 0.000068.
Values sent between devices are 32-bit elements; how exact they have to be, the bound alone decides.
No kernel may reach another device: no remote copies, remote signals or barrier semaphores. Data moves between devices by JAX's collectives and lax.ppermute only.
A program may use at most 64 MiB of HBM per device.

```python
import jax
import jax.numpy as jnp
from jax import lax

NB = 256
LC = 2
LR = 4
N = 4096
N_ROW = 4
N_COL = 8


def draw_matrix(key, part):
    gauss = jax.random.normal(key, (N, N), jnp.float32)
    symmetric = (gauss + gauss.T) * 0.70710678
    return symmetric.reshape(LR, N_ROW, NB, LC, N_COL, NB)


def draw_t_factor(key, part):
    upper_part = jax.random.normal(key, (NB, NB), jnp.float32)
    upper_part = upper_part * NB ** (-0.5)
    diagonal_vals = jax.random.uniform(jax.random.fold_in(key, 3), (NB,), jnp.float32, 0.5, 1.5)
    return jnp.triu(upper_part, 1) + jnp.diag(diagonal_vals)


def block_levels(own_key, shape, shards, low, high):
    def one(axis_at, blocks):
        steps = jax.random.uniform(jax.random.fold_in(jax.random.fold_in(own_key, 6), axis_at), (blocks,), jnp.float32, low / len(shards), high / len(shards))
        return jnp.repeat(jnp.exp(steps), shape[axis_at] // blocks).reshape((-1,) + (1,) * (len(shape) - axis_at - 1))

    loudness = one(*shards[0])
    for cut in shards[1:]:
        loudness = loudness * one(*cut)
    return loudness


def noise(rng, extent, scale, reach, pieces=(), held_as=jnp.bfloat16):
    factor_of = block_levels(rng, extent, pieces, -0.22, 0.18) if pieces else 1.0
    values = jax.random.normal(rng, extent, jnp.float32) * scale * factor_of
    return jnp.minimum(jnp.maximum(values, -reach), reach).astype(held_as)


def setup_inputs(seed: int = 0) -> dict:
    splits = jax.random.split(jax.random.key(seed), 4)
    return {
        "matrix": draw_matrix(jax.random.fold_in(splits[3], 71), 0),
        "vectors": noise(splits[1], (LR, N_ROW, NB, NB), N ** -0.5, 0.09375, ((1, 4),), jnp.float32),
        "t_factor": draw_t_factor(jax.random.fold_in(splits[3], 71), 0),
    }


def product(left, right):
    return jnp.dot(left, right, precision=lax.Precision.HIGHEST, preferred_element_type=jnp.float32)


def reference(matrix, vectors, t_factor):
    matrix_full = matrix.reshape(N, N)
    vec_all = vectors.reshape(N, NB)
    top_block = jnp.tril(vec_all[:NB], -1) + jnp.eye(NB, dtype=vec_all.dtype)
    vec_all = jnp.concatenate([top_block, vec_all[NB:]], axis=0)
    applied = product(product(matrix_full, vec_all), t_factor)
    inner = product(vec_all.T, applied)
    middle = product(t_factor.T, inner)
    coupled = applied - 0.5 * product(vec_all, middle)
    result = matrix_full - product(vec_all, coupled.T) - product(coupled, vec_all.T)
    return result.reshape(matrix.shape)
```

```python
import functools

import jax
import jax.numpy as jnp
from jax import lax
from jax.experimental import pallas as pl
from jax.experimental.pallas import tpu as pltpu
from jax.sharding import PartitionSpec as P

AXES = ("row", "col")
F32, BF16 = jnp.float32, jnp.bfloat16
NN, NT, TN = ((1,), (0,)), ((1,), (1,)), ((0,), (0,))
LANES = 128
VMEM = pl.BlockSpec(memory_space=pltpu.VMEM)
HBM = pl.BlockSpec(memory_space=pltpu.HBM)


def split(value):
    high = value.astype(BF16)
    return high, (value - high.astype(F32)).astype(BF16)


def product(left, right, dims):
    def one(a, b):
        return lax.dot_general(a, b, (dims, ((), ())), preferred_element_type=F32)

    (lh, ll), (rh, rl) = left, right
    return one(lh, rh) + (one(lh, rl) + one(ll, rh))


def sds(*shape, dtype=F32):
    return jax.ShapeDtypeStruct(shape, dtype)


def call(kernel, outs, *args, specs=None, scratch=(), limit=32, flops=0):
    return pl.pallas_call(
        kernel,
        out_shape=outs,
        in_specs=specs or [VMEM] * len(args),
        out_specs=jax.tree.map(lambda _: VMEM, outs),
        scratch_shapes=list(scratch),
        compiler_params=pltpu.CompilerParams(vmem_limit_bytes=limit << 20),
        cost_estimate=pl.CostEstimate(flops=flops, bytes_accessed=1 << 20, transcendentals=0),
    )(*args)


def send(value, rows, cols, target):
    pairs = []
    for row in range(rows):
        for col in range(cols):
            to = target(row, col)
            if to is not None:
                pairs.append((row * cols + col, to[0] * cols + to[1]))
    return lax.ppermute(value, AXES, pairs)


def with_unit_top(block):
    size = block.shape[0]
    i = lax.broadcasted_iota(jnp.int32, (size, size), 0)
    j = lax.broadcasted_iota(jnp.int32, (size, size), 1)
    unit = jnp.where(i > j, block, jnp.where(i == j, 1.0, 0.0))
    return jnp.where(lax.axis_index("row") == 0, unit, block)


def tile_rows(ref, start, count, width, first, lanes):
    step = width // LANES
    return jnp.concatenate(
        [ref[pl.ds(start * step + first + k, count, stride=step), :] for k in range(lanes // LANES)], axis=1
    )


def sums_kernel(rows, cols, width, a_hbm, v_hbm, keep, give, own, a_buf, v_buf, a_sem, v_sem):
    nb = v_buf.shape[1]
    count, step, ratio = v_buf.shape[0], width // LANES, cols // rows
    core = lax.axis_index("row") % 2
    hi = lax.axis_index("col") // rows
    copies = []
    for b in range(count):
        v_copy = pltpu.make_async_copy(v_hbm.at[pl.ds(b * nb, nb)], v_buf.at[b], v_sem.at[b])
        a_copy = pltpu.make_async_copy(a_hbm.at[pl.ds(b * nb * step, nb * step)], a_buf.at[b], a_sem.at[b])
        v_copy.start()
        a_copy.start()
        copies.append((v_copy, a_copy))
    for b in range(count):
        copies[b][0].wait()
        block = v_buf[b]
        if b == 0:
            block = with_unit_top(block)

        @pl.when(hi == b % ratio)
        def _():
            own[pl.ds(b // ratio * nb, nb), :] = block

        right = split(block)
        copies[b][1].wait()
        for out, half in ((give, 1 - core), (keep, core)):
            left = split(tile_rows(a_buf.at[b], 0, nb, width, half * (nb // LANES), nb))
            value = product(left, right, TN)
            out[...] = value if b == 0 else out[...] + value


def chip_kernel(keep, came, chip, *parts):
    y = lax.axis_index("row") // 2
    chip[...] = keep[...] + came[...]
    piece = parts[0].shape[0]
    for s, part in enumerate(parts):
        part[...] = chip[pl.ds((y ^ s) * piece, piece), :]


def cols_kernel(near, over, t_ref, vecs, high, low):
    same = lax.axis_index("row") % 2 == lax.axis_index("col") % 2

    @pl.when(same)
    def _():
        vecs[...] = near[...]

    @pl.when(jnp.logical_not(same))
    def _():
        vecs[...] = over[...]

    high[...], low[...] = split(product(split(vecs[...]), split(t_ref[...]), NT))


def rows_kernel(v_ref, t_ref, high, low):
    nb = t_ref.shape[0]
    right = split(t_ref[...])
    for b in range(v_ref.shape[0] // nb):
        at = pl.ds(b * nb, nb)
        block = v_ref[at, :]
        if b == 0:
            block = with_unit_top(block)
        high[at, :], low[at, :] = split(product(split(block), right, NT))


def inner_kernel(mine, other, vecs, out, whole):
    half, count = mine.shape[0], out.shape[0]
    row = lax.axis_index("row")
    core = row % 2
    whole[...] = product(split(vecs[pl.ds(core * half, half), :]), split(mine[...]), TN) + product(
        split(vecs[pl.ds((1 - core) * half, half), :]), split(other[...]), TN
    )
    out[...] = whole[pl.ds(row * count, count), :]


def first_kernel(flip, pieces, nb, a_ref, u_high, u_low, *refs):
    *arrays, out, p_high, p_low = refs
    col = lax.axis_index("col")
    z, h = col // 2, (col % 2) ^ flip
    width, count = out.shape[1], out.shape[0]
    for array, at, s, piece in pieces:
        to = pl.ds((z ^ s) * piece, piece)
        p_high[to, :], p_low[to, :] = split(arrays[array][pl.ds(at, piece), :])
    right = u_high[...], u_low[...]
    for b in range(count // nb):
        at = pl.ds(b * nb, nb)
        value = product((p_high[at, :], p_low[at, :]), right, NT)
        out[at, :] = tile_rows(a_ref, h * count + b * nb, nb, width, 0, width) - value


def last_kernel(ys, nb, one, two, v_high, v_low, u_high, u_low, p_mine, p_other, *refs):
    *inners, out, inner, mixed, buf, sem = refs
    row, x = lax.axis_index("row"), lax.axis_index("col") % 2
    y, core = row // 2, row % 2
    count = inners[0].shape[0]
    for s in range(ys):
        inner[pl.ds(((y ^ s) * 2 + core) * count, count), :] = inners[s][...]
        inner[pl.ds(((y ^ s) * 2 + 1 - core) * count, count), :] = inners[ys][pl.ds(s * count, count), :]
    mixed[...] = product((u_high[...], u_low[...]), split(inner[...]), NT)
    half = p_mine.shape[0]
    for ref, c in ((p_mine, core), (p_other, 1 - core)):
        at = pl.ds(c * half, half)
        mixed[at, :] = mixed[at, :] - ref[...]
    right = split(mixed[...])
    width = one.shape[1]
    step = width // LANES
    blocks = one.shape[0] // nb
    copies = []
    for u, base in enumerate((one, two)):
        for b in range(blocks):
            at = (x ^ u) * blocks + b
            rows = pl.ds(at * nb, nb)
            value = base[pl.ds(b * nb, nb), :] + product((v_high[rows, :], v_low[rows, :]), right, NT)
            slot = u * blocks + b
            for k in range(step):
                buf[slot, pl.ds(k, nb, stride=step), :] = value[:, k * LANES : (k + 1) * LANES]
            copy = pltpu.make_async_copy(buf.at[slot], out.at[pl.ds(at * nb * step, nb * step)], sem.at[slot])
            copy.start()
            copies.append(copy)
    for copy in copies:
        copy.wait()


def per_device(matrix, vectors, t_factor):
    block_rows, _, nb, _ = vectors.shape
    width = matrix.shape[3] * nb
    rows, cols = lax.axis_size("row"), lax.axis_size("col")
    ratio, ys, zs = cols // rows, rows // 2, cols // 2
    row, col = lax.axis_index("row"), lax.axis_index("col")
    height, half, piece, share = block_rows * nb, width // 2, width // rows, nb // rows
    assert half == nb and block_rows == 2 * ratio
    step = width // LANES
    linear = matrix.reshape(height * step, LANES)
    vecs = vectors.reshape(height, nb)

    def move(value, target):
        return send(value, rows, cols, target)

    def other_core(r, c):
        return r ^ 1, c

    keep, give, own = call(
        functools.partial(sums_kernel, rows, cols, width),
        (sds(half, nb), sds(half, nb), sds(width, nb)),
        linear,
        vecs,
        specs=[HBM, HBM],
        scratch=[
            pltpu.VMEM((block_rows, nb * step, LANES), F32),
            pltpu.VMEM((block_rows, nb, nb), F32),
            pltpu.SemaphoreType.DMA((block_rows,)),
            pltpu.SemaphoreType.DMA((block_rows,)),
        ],
        limit=60,
    )
    chip, *parts = call(
        chip_kernel, [sds(half, nb)] + [sds(piece, nb)] * ys, keep, move(give, other_core)
    )

    shard = sum(
        move(part, lambda r, c, s=s: (c % rows, (c // rows) * rows + ((r // 2) ^ s) * 2 + r % 2))
        for s, part in enumerate(parts)
    )

    came = sum(move(own, lambda r, c, s=s: (r ^ (2 * s), c) if r == c % rows else None) for s in range(1, ys))
    near = jnp.where(row == col % rows, own, came)
    over = move(near, lambda r, c: other_core(r, c) if r % 2 == c % 2 else None)
    col_vecs, u_high, u_low = call(
        cols_kernel,
        (sds(width, nb), sds(width, nb, dtype=BF16), sds(width, nb, dtype=BF16)),
        near,
        over,
        t_factor,
    )
    v_high, v_low = call(
        rows_kernel, (sds(height, nb, dtype=BF16), sds(height, nb, dtype=BF16)), vecs, t_factor
    )

    mine = chip + sum(move(chip, lambda r, c, s=s: (r ^ (2 * s), c)) for s in range(1, ys))
    other = move(mine, other_core)

    inner = call(inner_kernel, sds(share, nb), mine, other, col_vecs, scratch=[pltpu.VMEM((nb, nb), F32)])
    inner = inner + sum(move(inner, lambda r, c, s=s: (r, c ^ (2 * s))) for s in range(1, zs))
    inner = inner + move(inner, lambda r, c: (r, c ^ 1))
    inners = [inner] + [move(inner, lambda r, c, s=s: (r ^ (2 * s), c)) for s in range(1, ys)]
    inners.append(move(jnp.concatenate(inners, axis=0), other_core))

    along = [shard] + [move(shard, lambda r, c, s=s: (r, c ^ (2 * s))) for s in range(1, zs)]
    early = move(jnp.concatenate(along[: zs // 2], axis=0), lambda r, c: (r, c ^ 1))
    late = move(jnp.concatenate(along[zs // 2 :], axis=0), lambda r, c: (r, c ^ 1))

    def first(flip, pieces, arrays):
        return call(
            functools.partial(first_kernel, flip, pieces, nb),
            sds(height // 2, width),
            linear,
            u_high,
            u_low,
            *arrays,
            scratch=[pltpu.VMEM((height // 2, nb), BF16)] * 2,
        )

    one = first(0, [(s, 0, s, piece) for s in range(zs)], along)
    two = first(1, [(2 * s // zs, s % (zs // 2) * piece, s, piece) for s in range(zs)], [early, late])

    result = pl.pallas_call(
        functools.partial(last_kernel, ys, nb),
        out_shape=sds(height * step, LANES),
        in_specs=[VMEM] * (8 + ys + 1),
        out_specs=HBM,
        scratch_shapes=[
            pltpu.VMEM((nb, nb), F32),
            pltpu.VMEM((width, nb), F32),
            pltpu.VMEM((block_rows, nb * step, LANES), F32),
            pltpu.SemaphoreType.DMA((block_rows,)),
        ],
        compiler_params=pltpu.CompilerParams(vmem_limit_bytes=32 << 20),
    )(one, two, v_high, v_low, u_high, u_low, mine, other, *inners)
    return result.reshape(matrix.shape)


def solution(mesh):
    in_specs = (P(None, "row", None, None, "col", None), P(None, "row", None, None), P())
    out_specs = P(None, "row", None, None, "col", None)
    return jax.shard_map(
        per_device, mesh=mesh, in_specs=in_specs, out_specs=out_specs, check_vma=False
    )
```

```python
import functools

import jax
import jax.numpy as jnp
from jax import lax
from jax.experimental import pallas as pl
from jax.experimental.pallas import tpu as pltpu
from jax.sharding import PartitionSpec as P

AXES = ("row", "col")
F32, BF16 = jnp.float32, jnp.bfloat16
NN, NT, TN = ((1,), (0,)), ((1,), (1,)), ((0,), (0,))
LANES = 128
VMEM = pl.BlockSpec(memory_space=pltpu.VMEM)
HBM = pl.BlockSpec(memory_space=pltpu.HBM)
ANY = pl.BlockSpec(memory_space=pl.ANY)


def split(value):
    high = value.astype(BF16)
    return high, (value - high.astype(F32)).astype(BF16)


def product(left, right, dims):
    def one(a, b):
        return lax.dot_general(a, b, (dims, ((), ())), preferred_element_type=F32)

    (lh, ll), (rh, rl) = left, right
    return one(lh, rh) + (one(lh, rl) + one(ll, rh))


def sds(*shape, dtype=F32):
    return jax.ShapeDtypeStruct(shape, dtype)


def call(kernel, outs, *args, specs=None, scratch=(), limit=32):
    return pl.pallas_call(
        kernel,
        out_shape=outs,
        in_specs=specs or [VMEM] * len(args),
        out_specs=jax.tree.map(lambda _: VMEM, outs),
        scratch_shapes=list(scratch),
        compiler_params=pltpu.CompilerParams(vmem_limit_bytes=limit << 20),
    )(*args)


def send(value, rows, cols, target):
    pairs = []
    for row in range(rows):
        for col in range(cols):
            to = target(row, col)
            if to is not None:
                pairs.append((row * cols + col, to[0] * cols + to[1]))
    return lax.ppermute(value, AXES, pairs)


def with_unit_top(block):
    size = block.shape[0]
    i = lax.broadcasted_iota(jnp.int32, (size, size), 0)
    j = lax.broadcasted_iota(jnp.int32, (size, size), 1)
    unit = jnp.where(i > j, block, jnp.where(i == j, 1.0, 0.0))
    return jnp.where(lax.axis_index("row") == 0, unit, block)


def tile_rows(ref, start, count, width, first, lanes):
    step = width // LANES
    return jnp.concatenate(
        [ref[pl.ds(start * step + first + k, count, stride=step), :] for k in range(lanes // LANES)], axis=1
    )


def sums_kernel(width, a_hbm, v_hbm, keep, give, a_buf, v_buf, a_sem, v_sem):
    nb = v_buf.shape[1]
    count, step = v_buf.shape[0], width // LANES
    core = lax.axis_index("row") % 2
    copies = []
    for b in range(count):
        v_copy = pltpu.make_async_copy(v_hbm.at[pl.ds(b * nb, nb)], v_buf.at[b], v_sem.at[b])
        a_copy = pltpu.make_async_copy(a_hbm.at[pl.ds(b * nb * step, nb * step)], a_buf.at[b], a_sem.at[b])
        v_copy.start()
        a_copy.start()
        copies.append((v_copy, a_copy))
    for b in range(count):
        copies[b][0].wait()
        block = v_buf[b]
        if b == 0:
            block = with_unit_top(block)
        right = split(block)
        copies[b][1].wait()
        for out, half in ((give, 1 - core), (keep, core)):
            left = split(tile_rows(a_buf.at[b], 0, nb, width, half * (nb // LANES), nb))
            value = product(left, right, TN)
            out[...] = value if b == 0 else out[...] + value


def add_kernel(*refs):
    *terms, out = refs
    total = terms[0][...]
    for term in terms[1:]:
        total = total + term[...]
    out[...] = total


def late_add_kernel(count, *refs):
    add_kernel(*refs[count:])


def own_kernel(rows, v_ref, out):
    nb = v_ref.shape[1]
    group, ratio = lax.axis_index("col") // rows, lax.axis_size("col") // rows
    for k in range(out.shape[0] // nb):
        block = v_ref[pl.ds((k * ratio + group) * nb, nb), :]
        if k == 0:
            block = jnp.where(group == 0, with_unit_top(block), block)
        out[pl.ds(k * nb, nb), :] = block


def near_kernel(blocks, own, *refs):
    vecs, outs = refs[:-blocks], refs[-blocks:]
    nb = outs[0].shape[0]
    home = lax.axis_index("row") == lax.axis_index("col") % lax.axis_size("row")
    for k, out in enumerate(outs):
        at = pl.ds(k * nb, nb)

        @pl.when(home)
        def _():
            out[...] = own[at, :]

        @pl.when(jnp.logical_not(home))
        def _():
            came = vecs[0][at, :]
            for ref in vecs[1:]:
                came = came + ref[at, :]
            out[...] = came


def cols_kernel(t_ref, *refs):
    *vecs, high, low = refs
    blocks = len(vecs) // 2
    nb = vecs[0].shape[0]
    same = lax.axis_index("row") % 2 == lax.axis_index("col") % 2
    right = split(t_ref[...])
    for k in range(blocks):
        at = pl.ds(k * nb, nb)
        block = jnp.where(same, vecs[k][...], vecs[blocks + k][...])
        high[at, :], low[at, :] = split(product(split(block), right, NT))


def part_kernel(t, rows, v_ref, p_one, p_two, *refs):
    *before, out = refs
    nb, ratio = out.shape[0], v_ref.shape[0] // out.shape[0] // 2
    col = lax.axis_index("col")
    group, x = col // rows, col % 2
    value = 0.0
    for k, array in enumerate((p_one, p_two)):
        at = (x ^ k) * ratio + (group ^ t)
        block = v_ref[pl.ds(at * nb, nb), :]
        block = jnp.where(at == 0, with_unit_top(block), block)
        value = value + product(split(block), split(array[...]), TN)
    for ref in before:
        value = value + ref[...]
    out[...] = value


def cut_kernel(t, rows, v_ref, p_one, p_two, before, keep, give, whole):
    part_kernel(t, rows, v_ref, p_one, p_two, before, whole)
    count = keep.shape[0]
    core = lax.axis_index("row") % 2
    keep[...] = whole[pl.ds(core * count, count), :]
    give[...] = whole[pl.ds((1 - core) * count, count), :]


def rows_kernel(v_ref, t_ref, high, low):
    nb = t_ref.shape[0]
    right = split(t_ref[...])
    for b in range(v_ref.shape[0] // nb):
        at = pl.ds(b * nb, nb)
        block = v_ref[at, :]
        if b == 0:
            block = with_unit_top(block)
        high[at, :], low[at, :] = split(product(split(block), right, NT))


def first_kernel(flip, rows, a_ref, u_high, u_low, *refs):
    *arrays, out = refs
    col = lax.axis_index("col")
    group, h = col // rows, (col % 2) ^ flip
    nb, width = arrays[0].shape[0], out.shape[1]
    right = u_high[...], u_low[...]
    for t, array in enumerate(arrays):
        at = group ^ t
        value = product(split(array[...]), right, NT)
        out[pl.ds(at * nb, nb), :] = tile_rows(a_ref, (h * len(arrays) + at) * nb, nb, width, 0, width) - value


def last_kernel(nb, one, two, v_high, v_low, u_high, u_low, p_mine, p_other, s_mine, s_other, out, *scratch):
    inner, mixed, buf, sem = scratch
    row, x = lax.axis_index("row"), lax.axis_index("col") % 2
    core = row % 2
    count = s_mine.shape[0]
    inner[pl.ds(core * count, count), :] = s_mine[...]
    inner[pl.ds((1 - core) * count, count), :] = s_other[...]
    mixed[...] = product((u_high[...], u_low[...]), split(inner[...]), NT)
    half = p_mine.shape[0]
    for ref, c in ((p_mine, core), (p_other, 1 - core)):
        at = pl.ds(c * half, half)
        mixed[at, :] = mixed[at, :] - ref[...]
    right = split(mixed[...])
    width = one.shape[1]
    step = width // LANES
    blocks = one.shape[0] // nb
    copies = []
    for u, base in enumerate((one, two)):
        for b in range(blocks):
            at = (x ^ u) * blocks + b
            rows = pl.ds(at * nb, nb)
            value = base[pl.ds(b * nb, nb), :] + product((v_high[rows, :], v_low[rows, :]), right, NT)
            slot = u * blocks + b
            for k in range(step):
                buf[slot, pl.ds(k, nb, stride=step), :] = value[:, k * LANES : (k + 1) * LANES]
            copy = pltpu.make_async_copy(buf.at[slot], out.at[pl.ds(at * nb * step, nb * step)], sem.at[slot])
            copy.start()
            copies.append(copy)
    for copy in copies:
        copy.wait()


def per_device(matrix, vectors, t_factor):
    block_rows, _, nb, _ = vectors.shape
    width = matrix.shape[3] * nb
    rows, cols = lax.axis_size("row"), lax.axis_size("col")
    ratio, ys, zs = cols // rows, rows // 2, cols // 2
    row, col = lax.axis_index("row"), lax.axis_index("col")
    height, half, piece, share = block_rows * nb, width // 2, width // rows, nb // rows
    assert half == nb and block_rows == 2 * ratio
    step = width // LANES
    linear = matrix.reshape(height * step, LANES)
    vecs = vectors.reshape(height, nb)

    def move(value, target):
        return send(value, rows, cols, target)

    def other_core(r, c):
        return r ^ 1, c

    keep, give = call(
        functools.partial(sums_kernel, width),
        (sds(half, nb), sds(half, nb)),
        pltpu.with_memory_space_constraint(linear, pltpu.HBM),
        pltpu.with_memory_space_constraint(vecs, pltpu.HBM),
        specs=[HBM, HBM],
        scratch=[
            pltpu.VMEM((block_rows, nb * step, LANES), F32),
            pltpu.VMEM((block_rows, nb, nb), F32),
            pltpu.SemaphoreType.DMA((block_rows,)),
            pltpu.SemaphoreType.DMA((block_rows,)),
        ],
        limit=16,
    )
    chip = call(add_kernel, sds(half, nb), keep, move(give, other_core))

    sums = [move(chip, lambda r, c, s=s: (r ^ (2 * s), c)) for s in range(1, ys)]
    total = call(add_kernel, sds(half, nb), chip, *sums)

    def target(r, c, t):
        group, twin = c // rows, c % rows // 2
        return twin * 2 + c % 2, (group ^ t) * rows + (r ^ (2 * t))

    straight = [move(total, lambda r, c, t=t: target(r, c, t)) for t in range(ratio)]
    across = [move(value, lambda r, c: (r, c ^ 1)) for value in straight]

    own = call(functools.partial(own_kernel, rows), sds(width, nb), vecs)
    came = [move(own, lambda r, c, s=s: (r ^ (2 * s), c) if r == c % rows else None) for s in range(1, ys)]
    near = call(functools.partial(near_kernel, width // nb), [sds(nb, nb)] * (width // nb), own, *came)
    over = [move(part, lambda r, c: other_core(r, c) if r % 2 == c % 2 else None) for part in near]
    u_high, u_low = call(
        cols_kernel, (sds(width, nb, dtype=BF16), sds(width, nb, dtype=BF16)), t_factor, *near, *over
    )
    other = move(total, other_core)

    def first(flip, arrays):
        return call(
            functools.partial(first_kernel, flip, rows), sds(height // 2, width), linear, u_high, u_low, *arrays
        )

    one, two = first(0, straight), first(1, across)
    v_high, v_low = call(
        rows_kernel, (sds(height, nb, dtype=BF16), sds(height, nb, dtype=BF16)), vecs, t_factor
    )

    parts = []
    for t in range(ratio - 1):
        parts = [
            call(
                functools.partial(part_kernel, t, rows),
                sds(nb, nb),
                vecs,
                straight[t],
                across[t],
                *parts,
            )
        ]
    keep, give = call(
        functools.partial(cut_kernel, ratio - 1, rows),
        (sds(nb // 2, nb), sds(nb // 2, nb)),
        vecs,
        straight[-1],
        across[-1],
        *parts,
        scratch=[pltpu.VMEM((nb, nb), F32)],
    )
    share = call(add_kernel, sds(nb // 2, nb), keep, move(give, other_core))
    others = [move(share, lambda r, c, s=s: (r ^ (2 * s), c)) for s in range(1, ys)]
    ready = (one, two, v_high)
    share = call(
        functools.partial(late_add_kernel, len(ready)),
        sds(nb // 2, nb),
        *ready,
        share,
        *others,
        specs=[ANY] * len(ready) + [VMEM] * ys,
    )
    rest = move(share, other_core)

    result = pl.pallas_call(
        functools.partial(last_kernel, nb),
        out_shape=sds(height * step, LANES),
        in_specs=[VMEM] * 10,
        out_specs=HBM,
        scratch_shapes=[
            pltpu.VMEM((nb, nb), F32),
            pltpu.VMEM((width, nb), F32),
            pltpu.VMEM((block_rows, nb * step, LANES), F32),
            pltpu.SemaphoreType.DMA((block_rows,)),
        ],
        compiler_params=pltpu.CompilerParams(vmem_limit_bytes=32 << 20),
    )(one, two, v_high, v_low, u_high, u_low, total, other, share, rest)
    return result.reshape(matrix.shape)


def solution(mesh):
    in_specs = (P(None, "row", None, None, "col", None), P(None, "row", None, None), P())
    out_specs = P(None, "row", None, None, "col", None)
    return jax.shard_map(
        per_device, mesh=mesh, in_specs=in_specs, out_specs=out_specs, check_vma=False
    )
```

```python
import functools

import jax
import jax.numpy as jnp
from jax import lax
from jax.experimental import pallas as pl
from jax.experimental.pallas import tpu as pltpu
from jax.sharding import PartitionSpec as P

AXES = ("row", "col")
F32, BF16 = jnp.float32, jnp.bfloat16
NN, NT, TN = ((1,), (0,)), ((1,), (1,)), ((0,), (0,))
LANES = 128
VMEM = pl.BlockSpec(memory_space=pltpu.VMEM)
HBM = pl.BlockSpec(memory_space=pltpu.HBM)
ANY = pl.BlockSpec(memory_space=pl.ANY)


def split(value):
    high = value.astype(BF16)
    return high, (value - high.astype(F32)).astype(BF16)


def product(left, right, dims):
    def one(a, b):
        return lax.dot_general(a, b, (dims, ((), ())), preferred_element_type=F32)

    (lh, ll), (rh, rl) = left, right
    return one(lh, rh) + (one(lh, rl) + one(ll, rh))


def sds(*shape, dtype=F32):
    return jax.ShapeDtypeStruct(shape, dtype)


def call(kernel, outs, *args, specs=None, scratch=(), limit=32):
    return pl.pallas_call(
        kernel,
        out_shape=outs,
        in_specs=specs or [VMEM] * len(args),
        out_specs=jax.tree.map(lambda _: VMEM, outs),
        scratch_shapes=list(scratch),
        compiler_params=pltpu.CompilerParams(vmem_limit_bytes=limit << 20),
    )(*args)


def send(value, rows, cols, target):
    pairs = []
    for row in range(rows):
        for col in range(cols):
            to = target(row, col)
            if to is not None:
                pairs.append((row * cols + col, to[0] * cols + to[1]))
    return lax.ppermute(value, AXES, pairs)


def with_unit_top(block):
    size = block.shape[0]
    i = lax.broadcasted_iota(jnp.int32, (size, size), 0)
    j = lax.broadcasted_iota(jnp.int32, (size, size), 1)
    unit = jnp.where(i > j, block, jnp.where(i == j, 1.0, 0.0))
    return jnp.where(lax.axis_index("row") == 0, unit, block)


def tile_rows(ref, start, count, width, first, lanes):
    step = width // LANES
    return jnp.concatenate(
        [ref[pl.ds(start * step + first + k, count, stride=step), :] for k in range(lanes // LANES)], axis=1
    )


def sums_kernel(width, a_hbm, v_hbm, keep, give, a_buf, v_buf, a_sem, v_sem):
    nb = v_buf.shape[1]
    count, step = v_buf.shape[0], width // LANES
    core = lax.axis_index("row") % 2
    copies = []
    for b in range(count):
        v_copy = pltpu.make_async_copy(v_hbm.at[pl.ds(b * nb, nb)], v_buf.at[b], v_sem.at[b])
        a_copy = pltpu.make_async_copy(a_hbm.at[pl.ds(b * nb * step, nb * step)], a_buf.at[b], a_sem.at[b])
        v_copy.start()
        a_copy.start()
        copies.append((v_copy, a_copy))
    for b in range(count):
        copies[b][0].wait()
        block = v_buf[b]
        if b == 0:
            block = with_unit_top(block)
        right = split(block)
        copies[b][1].wait()
        for out, half in ((give, 1 - core), (keep, core)):
            left = split(tile_rows(a_buf.at[b], 0, nb, width, half * (nb // LANES), nb))
            value = product(left, right, TN)
            out[...] = value if b == 0 else out[...] + value


def add_kernel(*refs):
    *terms, out = refs
    total = terms[0][...]
    for term in terms[1:]:
        total = total + term[...]
    out[...] = total


def late_add_kernel(count, *refs):
    add_kernel(*refs[count:])


def late_add(ready, *terms):
    return call(
        functools.partial(late_add_kernel, len(ready)),
        sds(*terms[0].shape),
        *ready,
        *terms,
        specs=[ANY] * len(ready) + [VMEM] * len(terms),
    )


def own_kernel(rows, _, v_ref, *outs):
    nb = v_ref.shape[1]
    group, ratio = lax.axis_index("col") // rows, lax.axis_size("col") // rows
    core = lax.axis_index("row") % 2
    for k, out in zip((core, 1 - core), outs):
        at = k * ratio + group
        block = v_ref[pl.ds(at * nb, nb), :]
        out[...] = jnp.where(at == 0, with_unit_top(block), block)


def pick_core_kernel(mine, came, out):
    same = lax.axis_index("row") % 2 == lax.axis_index("col") % 2
    out[...] = jnp.where(same, mine[...], came[...])


def pick_plane_kernel(mine, *refs):
    *vecs, out = refs
    rows = lax.axis_size("row")
    same = lax.axis_index("row") // 2 == lax.axis_index("col") % rows // 2
    came = vecs[0][...]
    for ref in vecs[1:]:
        came = came + ref[...]
    out[...] = jnp.where(same, mine[...], came)


def cols_kernel(mine, other, t_ref, high, low):
    nb = mine.shape[0]
    core = lax.axis_index("row") % 2
    right = split(t_ref[...])
    for k, ref in zip((core, 1 - core), (mine, other)):
        at = pl.ds(k * nb, nb)
        high[at, :], low[at, :] = split(product(split(ref[...]), right, NT))


def part_kernel(rows, v_ref, *refs):
    *arrays, keep, give, whole = refs
    nb, half = whole.shape[0], whole.shape[0] // 2
    col, core = lax.axis_index("col"), lax.axis_index("row") % 2
    group, x = col // rows, col % 2
    value = 0.0
    for t, array in enumerate(arrays):
        at = x * len(arrays) + (group ^ t)
        block = v_ref[pl.ds(at * nb, nb), :]
        block = jnp.where(at == 0, with_unit_top(block), block)
        value = value + product(split(block), split(array[...]), TN)
    whole[...] = value
    for out, first in ((keep, core == 0), (give, core == 1)):
        out[pl.ds(0, half), :] = jnp.where(first, whole[:half, :half], whole[half:, half:])
        out[pl.ds(half, half // 2), :] = jnp.where(first, whole[: half // 2, half:], whole[half // 2 : half, half:])


def rows_kernel(v_ref, t_ref, high, low):
    nb = t_ref.shape[0]
    right = split(t_ref[...])
    for b in range(v_ref.shape[0] // nb):
        at = pl.ds(b * nb, nb)
        block = v_ref[at, :]
        if b == 0:
            block = with_unit_top(block)
        high[at, :], low[at, :] = split(product(split(block), right, NT))


def first_kernel(flip, t, rows, a_ref, u_high, u_low, prods, *refs):
    out = refs[-1]
    col = lax.axis_index("col")
    group, h = col // rows, (col % 2) ^ flip
    nb, width = out.shape
    at = h * (lax.axis_size("col") // rows) + (group ^ t)
    value = product(split(prods[...]), (u_high[...], u_low[...]), NT)
    out[...] = tile_rows(a_ref, at * nb, nb, width, 0, width) - value


def last_kernel(places, rows, v_high, v_low, u_high, u_low, p_mine, p_other, s_mine, s_other, *refs):
    *bases, out, inner, mixed, buf, sem = refs
    row, col = lax.axis_index("row"), lax.axis_index("col")
    core = row % 2
    half = inner.shape[0] // 2
    first = jnp.where(core == 0, s_mine[...], s_other[...])
    second = jnp.where(core == 0, s_other[...], s_mine[...])
    corner = jnp.concatenate([first[half:], second[half:]], axis=0)
    inner[:half, :half] = first[:half]
    inner[:half, half:] = corner
    inner[half:, :half] = corner.T
    inner[half:, half:] = second[:half]
    mixed[...] = product((u_high[...], u_low[...]), split(inner[...]), NT)
    half = p_mine.shape[0]
    for ref, c in ((p_mine, core), (p_other, 1 - core)):
        at = pl.ds(c * half, half)
        mixed[at, :] = mixed[at, :] - ref[...]
    right = split(mixed[...])
    nb, width = bases[0].shape
    step = width // LANES
    copies = []
    for k, (base, (flip, t)) in enumerate(zip(bases, places)):
        at = (col % 2 ^ flip) * (lax.axis_size("col") // rows) + (col // rows ^ t)
        rows_at = pl.ds(at * nb, nb)
        value = base[...] + product((v_high[rows_at, :], v_low[rows_at, :]), right, NT)
        for j in range(step):
            buf[k, pl.ds(j, nb, stride=step), :] = value[:, j * LANES : (j + 1) * LANES]
        copy = pltpu.make_async_copy(buf.at[k], out.at[pl.ds(at * nb * step, nb * step)], sem.at[k])
        copy.start()
        copies.append(copy)
    for copy in copies:
        copy.wait()


def per_device(matrix, vectors, t_factor):
    block_rows, _, nb, _ = vectors.shape
    width = matrix.shape[3] * nb
    rows, cols = lax.axis_size("row"), lax.axis_size("col")
    ratio, ys, zs = cols // rows, rows // 2, cols // 2
    row, col = lax.axis_index("row"), lax.axis_index("col")
    height, half, piece, share = block_rows * nb, width // 2, width // rows, nb // rows
    assert half == nb and block_rows == 2 * ratio
    step = width // LANES
    linear = matrix.reshape(height * step, LANES)
    vecs = vectors.reshape(height, nb)

    def move(value, target):
        return send(value, rows, cols, target)

    def other_core(r, c):
        return r ^ 1, c

    keep, give = call(
        functools.partial(sums_kernel, width),
        (sds(half, nb), sds(half, nb)),
        pltpu.with_memory_space_constraint(linear, pltpu.HBM),
        pltpu.with_memory_space_constraint(vecs, pltpu.HBM),
        specs=[HBM, HBM],
        scratch=[
            pltpu.VMEM((block_rows, nb * step, LANES), F32),
            pltpu.VMEM((block_rows, nb, nb), F32),
            pltpu.SemaphoreType.DMA((block_rows,)),
            pltpu.SemaphoreType.DMA((block_rows,)),
        ],
        limit=16,
    )
    chip = call(add_kernel, sds(half, nb), keep, move(give, other_core))

    sums = [move(chip, lambda r, c, s=s: (r ^ (2 * s), c)) for s in range(1, ys)]
    total = call(add_kernel, sds(half, nb), chip, *sums)

    def target(r, c, t):
        group, twin = c // rows, c % rows // 2
        return twin * 2 + c % 2, (group ^ t) * rows + (r ^ (2 * t))

    straight = [move(total, lambda r, c, t=t: target(r, c, t)) for t in range(ratio)]
    across = [move(value, lambda r, c: (r, c ^ 1)) for value in straight]

    own = call(functools.partial(own_kernel, rows), [sds(nb, nb)] * 2, keep, vecs, specs=[ANY, VMEM])
    came = move(own[1], lambda r, c: other_core(r, c) if r == c % rows else None)
    block = call(pick_core_kernel, sds(nb, nb), own[0], came)
    came = [
        move(block, lambda r, c, s=s: (r ^ (2 * s), c) if r // 2 == c % rows // 2 else None) for s in range(1, ys)
    ]
    near = call(pick_plane_kernel, sds(nb, nb), block, *came)
    u_high, u_low = call(
        cols_kernel,
        (sds(width, nb, dtype=BF16), sds(width, nb, dtype=BF16)),
        near,
        move(near, other_core),
        t_factor,
    )
    other = move(total, other_core)

    places = [(1, 0)] + [(0, t) for t in range(ratio)] + [(1, t) for t in range(1, ratio)]
    bases = []
    for flip, t in places:
        bases.append(
            call(
                functools.partial(first_kernel, flip, t, rows),
                sds(nb, width),
                linear,
                u_high,
                u_low,
                (straight, across)[flip][t],
                *bases[-1:],
                specs=[VMEM] * 4 + [ANY] * len(bases[-1:]),
            )
        )
    v_high, v_low = call(
        rows_kernel, (sds(height, nb, dtype=BF16), sds(height, nb, dtype=BF16)), vecs, t_factor
    )

    keep, give = call(
        functools.partial(part_kernel, rows),
        (sds(3 * nb // 4, nb // 2), sds(3 * nb // 4, nb // 2)),
        vecs,
        *straight,
        scratch=[pltpu.VMEM((nb, nb), F32)],
    )
    share = late_add((), keep, move(give, other_core))
    share = late_add(bases[ratio : ratio + 1], share, *[move(share, lambda r, c, s=s: (r ^ (2 * s), c)) for s in range(1, ys)])
    share = late_add((bases[-1], v_high), share, move(share, lambda r, c: (r, c ^ 1)))
    rest = move(share, other_core)

    result = pl.pallas_call(
        functools.partial(last_kernel, places, rows),
        out_shape=sds(height * step, LANES),
        in_specs=[VMEM] * (8 + len(bases)),
        out_specs=HBM,
        scratch_shapes=[
            pltpu.VMEM((nb, nb), F32),
            pltpu.VMEM((width, nb), F32),
            pltpu.VMEM((block_rows, nb * step, LANES), F32),
            pltpu.SemaphoreType.DMA((block_rows,)),
        ],
        compiler_params=pltpu.CompilerParams(vmem_limit_bytes=32 << 20),
    )(v_high, v_low, u_high, u_low, total, other, share, rest, *bases)
    return result.reshape(matrix.shape)


def solution(mesh):
    in_specs = (P(None, "row", None, None, "col", None), P(None, "row", None, None), P())
    out_specs = P(None, "row", None, None, "col", None)
    return jax.shard_map(
        per_device, mesh=mesh, in_specs=in_specs, out_specs=out_specs, check_vma=False
    )
```

```python
import functools

import jax
import jax.numpy as jnp
from jax import lax
from jax.experimental import pallas as pl
from jax.experimental.pallas import tpu as pltpu
from jax.sharding import PartitionSpec as P

AXES = ("row", "col")
F32, BF16 = jnp.float32, jnp.bfloat16
NN, NT, TN = ((1,), (0,)), ((1,), (1,)), ((0,), (0,))
LANES = 128
VMEM = pl.BlockSpec(memory_space=pltpu.VMEM)
HBM = pl.BlockSpec(memory_space=pltpu.HBM)
ANY = pl.BlockSpec(memory_space=pl.ANY)


def split(value):
    high = value.astype(BF16)
    return high, (value - high.astype(F32)).astype(BF16)


def product(left, right, dims):
    def one(a, b):
        return lax.dot_general(a, b, (dims, ((), ())), preferred_element_type=F32)

    (lh, ll), (rh, rl) = left, right
    return one(lh, rh) + (one(lh, rl) + one(ll, rh))


def sds(*shape, dtype=F32):
    return jax.ShapeDtypeStruct(shape, dtype)


def call(kernel, outs, *args, specs=None, scratch=(), limit=32):
    return pl.pallas_call(
        kernel,
        out_shape=outs,
        in_specs=specs or [VMEM] * len(args),
        out_specs=jax.tree.map(lambda _: VMEM, outs),
        scratch_shapes=list(scratch),
        compiler_params=pltpu.CompilerParams(vmem_limit_bytes=limit << 20),
    )(*args)


def send(value, rows, cols, target):
    pairs = []
    for row in range(rows):
        for col in range(cols):
            to = target(row, col)
            if to is not None:
                pairs.append((row * cols + col, to[0] * cols + to[1]))
    return lax.ppermute(value, AXES, pairs)


def with_unit_top(block):
    size = block.shape[0]
    i = lax.broadcasted_iota(jnp.int32, (size, size), 0)
    j = lax.broadcasted_iota(jnp.int32, (size, size), 1)
    unit = jnp.where(i > j, block, jnp.where(i == j, 1.0, 0.0))
    return jnp.where(lax.axis_index("row") == 0, unit, block)


def tile_rows(ref, start, count, width, first, lanes):
    step = width // LANES
    return jnp.concatenate(
        [ref[pl.ds(start * step + first + k, count, stride=step), :] for k in range(lanes // LANES)], axis=1
    )


def sums_kernel(width, a_hbm, v_hbm, keep, give, a_buf, v_buf, a_sem, v_sem):
    nb = v_buf.shape[1]
    count, step = v_buf.shape[0], width // LANES
    core = lax.axis_index("row") % 2
    copies = []
    for b in range(count):
        v_copy = pltpu.make_async_copy(v_hbm.at[pl.ds(b * nb, nb)], v_buf.at[b], v_sem.at[b])
        a_copy = pltpu.make_async_copy(a_hbm.at[pl.ds(b * nb * step, nb * step)], a_buf.at[b], a_sem.at[b])
        v_copy.start()
        a_copy.start()
        copies.append((v_copy, a_copy))
    for b in range(count):
        copies[b][0].wait()
        block = v_buf[b]
        if b == 0:
            block = with_unit_top(block)
        right = split(block)
        copies[b][1].wait()
        for out, half in ((give, 1 - core), (keep, core)):
            left = split(tile_rows(a_buf.at[b], 0, nb, width, half * (nb // LANES), nb))
            value = product(left, right, TN)
            out[...] = value if b == 0 else out[...] + value


def add_kernel(*refs):
    *terms, out = refs
    total = terms[0][...]
    for term in terms[1:]:
        total = total + term[...]
    out[...] = total


def total_kernel(*refs):
    *terms, out, upper, lower = refs
    add_kernel(*terms, out)
    half = upper.shape[0]
    upper[...] = out[:half]
    lower[...] = out[half:]


def join_kernel(upper, lower, out):
    half = upper.shape[0]
    out[:half] = upper[...]
    out[half:] = lower[...]


def late_add_kernel(count, *refs):
    add_kernel(*refs[count:])


def late_add(ready, *terms):
    return call(
        functools.partial(late_add_kernel, len(ready)),
        sds(*terms[0].shape),
        *ready,
        *terms,
        specs=[ANY] * len(ready) + [VMEM] * len(terms),
    )


def own_kernel(rows, _, v_ref, *outs):
    nb = v_ref.shape[1]
    group, ratio = lax.axis_index("col") // rows, lax.axis_size("col") // rows
    core = lax.axis_index("row") % 2
    for k, out in zip((core, 1 - core), outs):
        at = k * ratio + group
        block = v_ref[pl.ds(at * nb, nb), :]
        out[...] = jnp.where(at == 0, with_unit_top(block), block)


def pick_core_kernel(mine, came, out):
    same = lax.axis_index("row") % 2 == lax.axis_index("col") % 2
    out[...] = jnp.where(same, mine[...], came[...])


def pick_plane_kernel(mine, *refs):
    *vecs, out = refs
    rows = lax.axis_size("row")
    same = lax.axis_index("row") // 2 == lax.axis_index("col") % rows // 2
    came = vecs[0][...]
    for ref in vecs[1:]:
        came = came + ref[...]
    out[...] = jnp.where(same, mine[...], came)


def cols_kernel(mine, other, t_ref, high, low):
    nb = mine.shape[0]
    core = lax.axis_index("row") % 2
    right = split(t_ref[...])
    for k, ref in zip((core, 1 - core), (mine, other)):
        at = pl.ds(k * nb, nb)
        high[at, :], low[at, :] = split(product(split(ref[...]), right, NT))


def part_kernel(rows, v_ref, *refs):
    *arrays, keep, give, whole = refs
    nb, half = whole.shape[0], whole.shape[0] // 2
    col, core = lax.axis_index("col"), lax.axis_index("row") % 2
    group, x = col // rows, col % 2
    value = 0.0
    for t, array in enumerate(arrays):
        at = x * len(arrays) + (group ^ t)
        block = v_ref[pl.ds(at * nb, nb), :]
        block = jnp.where(at == 0, with_unit_top(block), block)
        value = value + product(split(block), split(array[...]), TN)
    whole[...] = value
    for out, first in ((keep, core == 0), (give, core == 1)):
        out[pl.ds(0, half), :] = jnp.where(first, whole[:half, :half], whole[half:, half:])
        out[pl.ds(half, half // 2), :] = jnp.where(first, whole[: half // 2, half:], whole[half // 2 : half, half:])


def rows_kernel(v_ref, t_ref, high, low):
    nb = t_ref.shape[0]
    right = split(t_ref[...])
    for b in range(v_ref.shape[0] // nb):
        at = pl.ds(b * nb, nb)
        block = v_ref[at, :]
        if b == 0:
            block = with_unit_top(block)
        high[at, :], low[at, :] = split(product(split(block), right, NT))


def first_kernel(flip, t, rows, a_ref, u_high, u_low, prods, *refs):
    out = refs[-1]
    col = lax.axis_index("col")
    group, h = col // rows, (col % 2) ^ flip
    nb, width = out.shape
    at = h * (lax.axis_size("col") // rows) + (group ^ t)
    value = product(split(prods[...]), (u_high[...], u_low[...]), NT)
    out[...] = tile_rows(a_ref, at * nb, nb, width, 0, width) - value


def last_kernel(places, rows, v_high, v_low, u_high, u_low, p_mine, p_other, s_mine, s_other, *refs):
    *bases, out, inner, mixed, buf, sem = refs
    row, col = lax.axis_index("row"), lax.axis_index("col")
    core = row % 2
    half = inner.shape[0] // 2
    first = jnp.where(core == 0, s_mine[...], s_other[...])
    second = jnp.where(core == 0, s_other[...], s_mine[...])
    corner = jnp.concatenate([first[half:], second[half:]], axis=0)
    inner[:half, :half] = first[:half]
    inner[:half, half:] = corner
    inner[half:, :half] = corner.T
    inner[half:, half:] = second[:half]
    mixed[...] = product((u_high[...], u_low[...]), split(inner[...]), NT)
    half = p_mine.shape[0]
    for ref, c in ((p_mine, core), (p_other, 1 - core)):
        at = pl.ds(c * half, half)
        mixed[at, :] = mixed[at, :] - ref[...]
    right = split(mixed[...])
    nb, width = bases[0].shape
    step = width // LANES
    copies = []
    for k, (base, (flip, t)) in enumerate(zip(bases, places)):
        at = (col % 2 ^ flip) * (lax.axis_size("col") // rows) + (col // rows ^ t)
        rows_at = pl.ds(at * nb, nb)
        value = base[...] + product((v_high[rows_at, :], v_low[rows_at, :]), right, NT)
        for j in range(step):
            buf[k, pl.ds(j, nb, stride=step), :] = value[:, j * LANES : (j + 1) * LANES]
        copy = pltpu.make_async_copy(buf.at[k], out.at[pl.ds(at * nb * step, nb * step)], sem.at[k])
        copy.start()
        copies.append(copy)
    for copy in copies:
        copy.wait()


def per_device(matrix, vectors, t_factor):
    block_rows, _, nb, _ = vectors.shape
    width = matrix.shape[3] * nb
    rows, cols = lax.axis_size("row"), lax.axis_size("col")
    ratio, ys, zs = cols // rows, rows // 2, cols // 2
    row, col = lax.axis_index("row"), lax.axis_index("col")
    height, half, piece, share = block_rows * nb, width // 2, width // rows, nb // rows
    assert half == nb and block_rows == 2 * ratio
    step = width // LANES
    linear = matrix.reshape(height * step, LANES)
    vecs = vectors.reshape(height, nb)

    def move(value, target):
        return send(value, rows, cols, target)

    def other_core(r, c):
        return r ^ 1, c

    keep, give = call(
        functools.partial(sums_kernel, width),
        (sds(half, nb), sds(half, nb)),
        pltpu.with_memory_space_constraint(linear, pltpu.HBM),
        pltpu.with_memory_space_constraint(vecs, pltpu.HBM),
        specs=[HBM, HBM],
        scratch=[
            pltpu.VMEM((block_rows, nb * step, LANES), F32),
            pltpu.VMEM((block_rows, nb, nb), F32),
            pltpu.SemaphoreType.DMA((block_rows,)),
            pltpu.SemaphoreType.DMA((block_rows,)),
        ],
        limit=16,
    )
    chip = call(add_kernel, sds(half, nb), keep, move(give, other_core))

    sums = [move(chip, lambda r, c, s=s: (r ^ (2 * s), c)) for s in range(1, ys)]
    total, *halves = call(total_kernel, [sds(half, nb)] + [sds(half // 2, nb)] * 2, chip, *sums)

    def target(r, c, t):
        group, twin = c // rows, c % rows // 2
        return twin * 2 + c % 2, (group ^ t) * rows + (r ^ (2 * t))

    straight = [move(total, lambda r, c, t=t: target(r, c, t)) for t in range(1, ratio)]
    straight.insert(
        0, call(join_kernel, sds(half, nb), *[move(value, lambda r, c: target(r, c, 0)) for value in halves])
    )
    across = [move(value, lambda r, c: (r, c ^ 1)) for value in straight]

    own = call(functools.partial(own_kernel, rows), [sds(nb, nb)] * 2, keep, vecs, specs=[ANY, VMEM])
    came = move(own[1], lambda r, c: other_core(r, c) if r == c % rows else None)
    block = call(pick_core_kernel, sds(nb, nb), own[0], came)
    came = [
        move(block, lambda r, c, s=s: (r ^ (2 * s), c) if r // 2 == c % rows // 2 else None) for s in range(1, ys)
    ]
    near = call(pick_plane_kernel, sds(nb, nb), block, *came)
    u_high, u_low = call(
        cols_kernel,
        (sds(width, nb, dtype=BF16), sds(width, nb, dtype=BF16)),
        near,
        move(near, other_core),
        t_factor,
    )
    other = move(total, other_core)

    places = [(1, 0)] + [(0, t) for t in range(ratio)] + [(1, t) for t in range(1, ratio)]
    bases = []
    for flip, t in places:
        bases.append(
            call(
                functools.partial(first_kernel, flip, t, rows),
                sds(nb, width),
                linear,
                u_high,
                u_low,
                (straight, across)[flip][t],
                *bases[-1:],
                specs=[VMEM] * 4 + [ANY] * len(bases[-1:]),
            )
        )
    v_high, v_low = call(
        rows_kernel, (sds(height, nb, dtype=BF16), sds(height, nb, dtype=BF16)), vecs, t_factor
    )

    keep, give = call(
        functools.partial(part_kernel, rows),
        (sds(3 * nb // 4, nb // 2), sds(3 * nb // 4, nb // 2)),
        vecs,
        *straight,
        scratch=[pltpu.VMEM((nb, nb), F32)],
    )
    share = late_add((), keep, move(give, other_core))
    share = late_add(bases[ratio : ratio + 1], share, *[move(share, lambda r, c, s=s: (r ^ (2 * s), c)) for s in range(1, ys)])
    share = late_add((bases[-1], v_high), share, move(share, lambda r, c: (r, c ^ 1)))
    rest = move(share, other_core)

    result = pl.pallas_call(
        functools.partial(last_kernel, places, rows),
        out_shape=sds(height * step, LANES),
        in_specs=[VMEM] * (8 + len(bases)),
        out_specs=HBM,
        scratch_shapes=[
            pltpu.VMEM((nb, nb), F32),
            pltpu.VMEM((width, nb), F32),
            pltpu.VMEM((block_rows, nb * step, LANES), F32),
            pltpu.SemaphoreType.DMA((block_rows,)),
        ],
        compiler_params=pltpu.CompilerParams(vmem_limit_bytes=32 << 20),
    )(v_high, v_low, u_high, u_low, total, other, share, rest, *bases)
    return result.reshape(matrix.shape)


def solution(mesh):
    in_specs = (P(None, "row", None, None, "col", None), P(None, "row", None, None), P())
    out_specs = P(None, "row", None, None, "col", None)
    return jax.shard_map(
        per_device, mesh=mesh, in_specs=in_specs, out_specs=out_specs, check_vma=False
    )
```

```python
import functools

import jax
import jax.numpy as jnp
from jax import lax
from jax.experimental import pallas as pl
from jax.experimental.pallas import tpu as pltpu
from jax.sharding import PartitionSpec as P

AXES = ("row", "col")
F32, BF16 = jnp.float32, jnp.bfloat16
NN, NT, TN = ((1,), (0,)), ((1,), (1,)), ((0,), (0,))
LANES = 128
VMEM = pl.BlockSpec(memory_space=pltpu.VMEM)
HBM = pl.BlockSpec(memory_space=pltpu.HBM)
ANY = pl.BlockSpec(memory_space=pl.ANY)


def split(value):
    high = value.astype(BF16)
    return high, (value - high.astype(F32)).astype(BF16)


def product(left, right, dims):
    def one(a, b):
        return lax.dot_general(a, b, (dims, ((), ())), preferred_element_type=F32)

    (lh, ll), (rh, rl) = left, right
    return one(lh, rh) + (one(lh, rl) + one(ll, rh))


def sds(*shape, dtype=F32):
    return jax.ShapeDtypeStruct(shape, dtype)


def call(kernel, outs, *args, specs=None, scratch=(), limit=32):
    return pl.pallas_call(
        kernel,
        out_shape=outs,
        in_specs=specs or [VMEM] * len(args),
        out_specs=jax.tree.map(lambda _: VMEM, outs),
        scratch_shapes=list(scratch),
        compiler_params=pltpu.CompilerParams(vmem_limit_bytes=limit << 20),
    )(*args)


def send(value, rows, cols, target):
    pairs = []
    for row in range(rows):
        for col in range(cols):
            to = target(row, col)
            if to is not None:
                pairs.append((row * cols + col, to[0] * cols + to[1]))
    return lax.ppermute(value, AXES, pairs)


def with_unit_top(block):
    size = block.shape[0]
    i = lax.broadcasted_iota(jnp.int32, (size, size), 0)
    j = lax.broadcasted_iota(jnp.int32, (size, size), 1)
    unit = jnp.where(i > j, block, jnp.where(i == j, 1.0, 0.0))
    return jnp.where(lax.axis_index("row") == 0, unit, block)


def tile_rows(ref, start, count, width, first, lanes):
    step = width // LANES
    return jnp.concatenate(
        [ref[pl.ds(start * step + first + k, count, stride=step), :] for k in range(lanes // LANES)], axis=1
    )


def sums_kernel(width, a_hbm, v_hbm, keep, give, a_buf, v_buf, a_sem, v_sem):
    nb = v_buf.shape[1]
    count, step = v_buf.shape[0], width // LANES
    core = lax.axis_index("row") % 2
    copies = []
    for b in range(count):
        v_copy = pltpu.make_async_copy(v_hbm.at[pl.ds(b * nb, nb)], v_buf.at[b], v_sem.at[b])
        a_copy = pltpu.make_async_copy(a_hbm.at[pl.ds(b * nb * step, nb * step)], a_buf.at[b], a_sem.at[b])
        v_copy.start()
        a_copy.start()
        copies.append((v_copy, a_copy))
    for b in range(count):
        copies[b][0].wait()
        block = v_buf[b]
        if b == 0:
            block = with_unit_top(block)
        right = split(block)
        copies[b][1].wait()
        for out, half in ((give, 1 - core), (keep, core)):
            left = split(tile_rows(a_buf.at[b], 0, nb, width, half * (nb // LANES), nb))
            value = product(left, right, TN)
            out[...] = value if b == 0 else out[...] + value


def add_kernel(*refs):
    *terms, out = refs
    total = terms[0][...]
    for term in terms[1:]:
        total = total + term[...]
    out[...] = total


def cut_kernel(keep, came, *parts):
    y, count = lax.axis_index("row") // 2, parts[0].shape[0]
    for s, part in enumerate(parts):
        at = pl.ds((y ^ s) * count, count)
        part[...] = keep[at, :] + came[at, :]


def join_kernel(*refs):
    *pieces, out = refs
    count = pieces[0].shape[0]
    y = lax.axis_index("col") % lax.axis_size("row") // 2
    for s, piece in enumerate(pieces):
        out[pl.ds((y ^ s) * count, count), :] = piece[...]


def late_add_kernel(count, *refs):
    add_kernel(*refs[count:])


def late_add(ready, *terms):
    return call(
        functools.partial(late_add_kernel, len(ready)),
        sds(*terms[0].shape),
        *ready,
        *terms,
        specs=[ANY] * len(ready) + [VMEM] * len(terms),
    )


def own_kernel(rows, _, v_ref, *outs):
    nb = v_ref.shape[1]
    group, ratio = lax.axis_index("col") // rows, lax.axis_size("col") // rows
    core = lax.axis_index("row") % 2
    for k, out in zip((core, 1 - core), outs):
        at = k * ratio + group
        block = v_ref[pl.ds(at * nb, nb), :]
        out[...] = jnp.where(at == 0, with_unit_top(block), block)


def pick_core_kernel(mine, came, out):
    same = lax.axis_index("row") % 2 == lax.axis_index("col") % 2
    out[...] = jnp.where(same, mine[...], came[...])


def pick_plane_kernel(mine, *refs):
    *vecs, out = refs
    rows = lax.axis_size("row")
    same = lax.axis_index("row") // 2 == lax.axis_index("col") % rows // 2
    came = vecs[0][...]
    for ref in vecs[1:]:
        came = came + ref[...]
    out[...] = jnp.where(same, mine[...], came)


def cols_kernel(mine, other, t_ref, high, low):
    nb = mine.shape[0]
    core = lax.axis_index("row") % 2
    right = split(t_ref[...])
    for k, ref in zip((core, 1 - core), (mine, other)):
        at = pl.ds(k * nb, nb)
        high[at, :], low[at, :] = split(product(split(ref[...]), right, NT))


def part_kernel(rows, v_ref, *refs):
    *arrays, keep, give, whole = refs
    nb, half = whole.shape[0], whole.shape[0] // 2
    col, core = lax.axis_index("col"), lax.axis_index("row") % 2
    group, x = col // rows, col % 2
    value = 0.0
    for t, array in enumerate(arrays):
        at = x * len(arrays) + (group ^ t)
        block = v_ref[pl.ds(at * nb, nb), :]
        block = jnp.where(at == 0, with_unit_top(block), block)
        value = value + product(split(block), split(array[...]), TN)
    whole[...] = value
    for out, first in ((keep, core == 0), (give, core == 1)):
        out[pl.ds(0, half), :] = jnp.where(first, whole[:half, :half], whole[half:, half:])
        out[pl.ds(half, half // 2), :] = jnp.where(first, whole[: half // 2, half:], whole[half // 2 : half, half:])


def rows_kernel(v_ref, t_ref, high, low):
    nb = t_ref.shape[0]
    right = split(t_ref[...])
    for b in range(v_ref.shape[0] // nb):
        at = pl.ds(b * nb, nb)
        block = v_ref[at, :]
        if b == 0:
            block = with_unit_top(block)
        high[at, :], low[at, :] = split(product(split(block), right, NT))


def first_kernel(flip, t, rows, a_ref, u_high, u_low, prods, *refs):
    out = refs[-1]
    col = lax.axis_index("col")
    group, h = col // rows, (col % 2) ^ flip
    nb, width = out.shape
    at = h * (lax.axis_size("col") // rows) + (group ^ t)
    value = product(split(prods[...]), (u_high[...], u_low[...]), NT)
    out[...] = tile_rows(a_ref, at * nb, nb, width, 0, width) - value


def last_kernel(places, rows, v_high, v_low, u_high, u_low, s_mine, s_other, *refs):
    *refs, out, inner, mixed, buf, sem = refs
    bases, prods = refs[: len(places)], refs[len(places) :]
    row, col = lax.axis_index("row"), lax.axis_index("col")
    core = row % 2
    half = inner.shape[0] // 2
    first = jnp.where(core == 0, s_mine[...], s_other[...])
    second = jnp.where(core == 0, s_other[...], s_mine[...])
    corner = jnp.concatenate([first[half:], second[half:]], axis=0)
    inner[:half, :half] = first[:half]
    inner[:half, half:] = corner
    inner[half:, :half] = corner.T
    inner[half:, half:] = second[:half]
    mixed[...] = product((u_high[...], u_low[...]), split(inner[...]), NT)
    count, ys = prods[0].shape[0], len(prods) // 2
    for k, ref in enumerate(prods):
        at = pl.ds(((core ^ k // ys) * ys + (row // 2 ^ k % ys)) * count, count)
        mixed[at, :] = mixed[at, :] - ref[...]
    right = split(mixed[...])
    nb, width = bases[0].shape
    step = width // LANES
    copies = []
    for k, (base, (flip, t)) in enumerate(zip(bases, places)):
        at = (col % 2 ^ flip) * (lax.axis_size("col") // rows) + (col // rows ^ t)
        rows_at = pl.ds(at * nb, nb)
        value = base[...] + product((v_high[rows_at, :], v_low[rows_at, :]), right, NT)
        for j in range(step):
            buf[k, pl.ds(j, nb, stride=step), :] = value[:, j * LANES : (j + 1) * LANES]
        copy = pltpu.make_async_copy(buf.at[k], out.at[pl.ds(at * nb * step, nb * step)], sem.at[k])
        copy.start()
        copies.append(copy)
    for copy in copies:
        copy.wait()


def per_device(matrix, vectors, t_factor):
    block_rows, _, nb, _ = vectors.shape
    width = matrix.shape[3] * nb
    rows, cols = lax.axis_size("row"), lax.axis_size("col")
    ratio, ys, zs = cols // rows, rows // 2, cols // 2
    row, col = lax.axis_index("row"), lax.axis_index("col")
    height, half, piece, share = block_rows * nb, width // 2, width // rows, nb // rows
    assert half == nb and block_rows == 2 * ratio
    step = width // LANES
    linear = matrix.reshape(height * step, LANES)
    vecs = vectors.reshape(height, nb)

    def move(value, target):
        return send(value, rows, cols, target)

    def other_core(r, c):
        return r ^ 1, c

    keep, give = call(
        functools.partial(sums_kernel, width),
        (sds(half, nb), sds(half, nb)),
        pltpu.with_memory_space_constraint(linear, pltpu.HBM),
        pltpu.with_memory_space_constraint(vecs, pltpu.HBM),
        specs=[HBM, HBM],
        scratch=[
            pltpu.VMEM((block_rows, nb * step, LANES), F32),
            pltpu.VMEM((block_rows, nb, nb), F32),
            pltpu.SemaphoreType.DMA((block_rows,)),
            pltpu.SemaphoreType.DMA((block_rows,)),
        ],
        limit=16,
    )
    piece = half // ys
    cuts = call(cut_kernel, [sds(piece, nb)] * ys, keep, move(give, other_core))

    def along_y(value):
        return [move(value, lambda r, c, s=s: (r ^ (2 * s), c)) for s in range(1, ys)]

    total = call(
        add_kernel,
        sds(piece, nb),
        cuts[0],
        *[move(cut, lambda r, c, s=s: (r ^ (2 * s), c)) for s, cut in enumerate(cuts) if s],
    )
    mine = [total, *along_y(total)]

    def target(r, c, t, s):
        group, twin = c // rows, c % rows // 2
        return twin * 2 + c % 2, (group ^ t) * rows + (r ^ (2 * s))

    straight = [
        call(
            join_kernel,
            sds(half, nb),
            *[move(total, lambda r, c, t=t, s=s: target(r, c, t, s)) for s in range(ys)],
        )
        for t in range(ratio)
    ]
    across = [move(value, lambda r, c: (r, c ^ 1)) for value in straight]

    own = call(functools.partial(own_kernel, rows), [sds(nb, nb)] * 2, keep, vecs, specs=[ANY, VMEM])
    came = move(own[1], lambda r, c: other_core(r, c) if r == c % rows else None)
    block = call(pick_core_kernel, sds(nb, nb), own[0], came)
    came = [
        move(block, lambda r, c, s=s: (r ^ (2 * s), c) if r // 2 == c % rows // 2 else None) for s in range(1, ys)
    ]
    near = call(pick_plane_kernel, sds(nb, nb), block, *came)
    u_high, u_low = call(
        cols_kernel,
        (sds(width, nb, dtype=BF16), sds(width, nb, dtype=BF16)),
        near,
        move(near, other_core),
        t_factor,
    )
    other = [move(value, other_core) for value in mine]

    places = [(1, 1)] + [(0, t) for t in range(ratio)] + [(1, t) for t in range(ratio) if t != 1]
    bases = []
    for flip, t in places:
        bases.append(
            call(
                functools.partial(first_kernel, flip, t, rows),
                sds(nb, width),
                linear,
                u_high,
                u_low,
                (straight, across)[flip][t],
                *bases[-1:],
                specs=[VMEM] * 4 + [ANY] * len(bases[-1:]),
            )
        )
    v_high, v_low = call(
        rows_kernel, (sds(height, nb, dtype=BF16), sds(height, nb, dtype=BF16)), vecs, t_factor
    )

    keep, give = call(
        functools.partial(part_kernel, rows),
        (sds(3 * nb // 4, nb // 2), sds(3 * nb // 4, nb // 2)),
        vecs,
        *straight,
        scratch=[pltpu.VMEM((nb, nb), F32)],
    )
    share = late_add((), keep, move(give, other_core))
    share = late_add(bases[ratio : ratio + 1], share, *along_y(share))
    share = late_add((bases[-1], v_high), share, move(share, lambda r, c: (r, c ^ 1)))
    rest = move(share, other_core)

    result = pl.pallas_call(
        functools.partial(last_kernel, places, rows),
        out_shape=sds(height * step, LANES),
        in_specs=[VMEM] * (6 + len(bases) + 2 * ys),
        out_specs=HBM,
        scratch_shapes=[
            pltpu.VMEM((nb, nb), F32),
            pltpu.VMEM((width, nb), F32),
            pltpu.VMEM((block_rows, nb * step, LANES), F32),
            pltpu.SemaphoreType.DMA((block_rows,)),
        ],
        compiler_params=pltpu.CompilerParams(vmem_limit_bytes=32 << 20),
    )(v_high, v_low, u_high, u_low, share, rest, *bases, *mine, *other)
    return result.reshape(matrix.shape)


def solution(mesh):
    in_specs = (P(None, "row", None, None, "col", None), P(None, "row", None, None), P())
    out_specs = P(None, "row", None, None, "col", None)
    return jax.shard_map(
        per_device, mesh=mesh, in_specs=in_specs, out_specs=out_specs, check_vma=False
    )
```

```python
import functools

import jax
import jax.numpy as jnp
from jax import lax
from jax.experimental import pallas as pl
from jax.experimental.pallas import tpu as pltpu
from jax.sharding import PartitionSpec as P

AXES = ("row", "col")
F32, BF16 = jnp.float32, jnp.bfloat16
NN, NT, TN = ((1,), (0,)), ((1,), (1,)), ((0,), (0,))
LANES = 128
VMEM = pl.BlockSpec(memory_space=pltpu.VMEM)
HBM = pl.BlockSpec(memory_space=pltpu.HBM)
ANY = pl.BlockSpec(memory_space=pl.ANY)


def split(value):
    high = value.astype(BF16)
    return high, (value - high.astype(F32)).astype(BF16)


def product(left, right, dims):
    def one(a, b):
        return lax.dot_general(a, b, (dims, ((), ())), preferred_element_type=F32)

    (lh, ll), (rh, rl) = left, right
    return one(lh, rh) + (one(lh, rl) + one(ll, rh))


def sds(*shape, dtype=F32):
    return jax.ShapeDtypeStruct(shape, dtype)


def call(kernel, outs, *args, specs=None, scratch=(), limit=32):
    return pl.pallas_call(
        kernel,
        out_shape=outs,
        in_specs=specs or [VMEM] * len(args),
        out_specs=jax.tree.map(lambda _: VMEM, outs),
        scratch_shapes=list(scratch),
        compiler_params=pltpu.CompilerParams(vmem_limit_bytes=limit << 20),
    )(*args)


def send(value, rows, cols, target):
    pairs = []
    for row in range(rows):
        for col in range(cols):
            to = target(row, col)
            if to is not None:
                pairs.append((row * cols + col, to[0] * cols + to[1]))
    return lax.ppermute(value, AXES, pairs)


def with_unit_top(block):
    size = block.shape[0]
    i = lax.broadcasted_iota(jnp.int32, (size, size), 0)
    j = lax.broadcasted_iota(jnp.int32, (size, size), 1)
    unit = jnp.where(i > j, block, jnp.where(i == j, 1.0, 0.0))
    return jnp.where(lax.axis_index("row") == 0, unit, block)


def tile_rows(ref, start, count, width, first, lanes):
    step = width // LANES
    return jnp.concatenate(
        [ref[pl.ds(start * step + first + k, count, stride=step), :] for k in range(lanes // LANES)], axis=1
    )


def sums_kernel(width, a_hbm, v_hbm, keep, give, a_buf, v_buf, a_sem, v_sem):
    nb = v_buf.shape[1]
    count, step = v_buf.shape[0], width // LANES
    core = lax.axis_index("row") % 2
    copies = []
    for b in range(count):
        v_copy = pltpu.make_async_copy(v_hbm.at[pl.ds(b * nb, nb)], v_buf.at[b], v_sem.at[b])
        a_copy = pltpu.make_async_copy(a_hbm.at[pl.ds(b * nb * step, nb * step)], a_buf.at[b], a_sem.at[b])
        v_copy.start()
        a_copy.start()
        copies.append((v_copy, a_copy))
    for b in range(count):
        copies[b][0].wait()
        block = v_buf[b]
        if b == 0:
            block = with_unit_top(block)
        right = split(block)
        copies[b][1].wait()
        for out, half in ((give, 1 - core), (keep, core)):
            left = split(tile_rows(a_buf.at[b], 0, nb, width, half * (nb // LANES), nb))
            value = product(left, right, TN)
            out[...] = value if b == 0 else out[...] + value


def add_kernel(*refs):
    *terms, out = refs
    total = terms[0][...]
    for term in terms[1:]:
        total = total + term[...]
    out[...] = total


def cut_kernel(keep, came, *parts):
    y, count = lax.axis_index("row") // 2, parts[0].shape[0]
    for s, part in enumerate(parts):
        at = pl.ds((y ^ s) * count, count)
        part[...] = keep[at, :] + came[at, :]


def join_kernel(*refs):
    *pieces, out = refs
    count = pieces[0].shape[0]
    y = lax.axis_index("col") % lax.axis_size("row") // 2
    for s, piece in enumerate(pieces):
        out[pl.ds((y ^ s) * count, count), :] = piece[...]


def late_add_kernel(count, *refs):
    add_kernel(*refs[count:])


def late_add(ready, *terms):
    return call(
        functools.partial(late_add_kernel, len(ready)),
        sds(*terms[0].shape),
        *ready,
        *terms,
        specs=[ANY] * len(ready) + [VMEM] * len(terms),
    )


def own_kernel(rows, _, v_ref, *outs):
    nb = v_ref.shape[1]
    group, ratio = lax.axis_index("col") // rows, lax.axis_size("col") // rows
    core = lax.axis_index("row") % 2
    for k, out in zip((core, 1 - core), outs):
        at = k * ratio + group
        block = v_ref[pl.ds(at * nb, nb), :]
        out[...] = jnp.where(at == 0, with_unit_top(block), block)


def pick_core_kernel(mine, came, out):
    same = lax.axis_index("row") % 2 == lax.axis_index("col") % 2
    out[...] = jnp.where(same, mine[...], came[...])


def pick_plane_kernel(mine, *refs):
    *vecs, out = refs
    rows = lax.axis_size("row")
    same = lax.axis_index("row") // 2 == lax.axis_index("col") % rows // 2
    came = vecs[0][...]
    for ref in vecs[1:]:
        came = came + ref[...]
    out[...] = jnp.where(same, mine[...], came)


def scale_kernel(v_ref, mine, other, t_ref, high, low, v_high, v_low):
    nb = mine.shape[0]
    core = lax.axis_index("row") % 2
    right = split(t_ref[...])
    for k, ref in zip((core, 1 - core), (mine, other)):
        at = pl.ds(k * nb, nb)
        high[at, :], low[at, :] = split(product(split(ref[...]), right, NT))
    for b in range(v_ref.shape[0] // nb):
        at = pl.ds(b * nb, nb)
        block = v_ref[at, :]
        if b == 0:
            block = with_unit_top(block)
        v_high[at, :], v_low[at, :] = split(product(split(block), right, NT))


def part_kernel(rows, v_ref, *refs):
    *arrays, keep, give, whole = refs
    nb, half = whole.shape[0], whole.shape[0] // 2
    col, core = lax.axis_index("col"), lax.axis_index("row") % 2
    group, x = col // rows, col % 2
    value = 0.0
    for t, array in enumerate(arrays):
        at = x * len(arrays) + (group ^ t)
        block = v_ref[pl.ds(at * nb, nb), :]
        block = jnp.where(at == 0, with_unit_top(block), block)
        value = value + product(split(block), split(array[...]), TN)
    whole[...] = value
    for out, first in ((keep, core == 0), (give, core == 1)):
        out[pl.ds(0, half), :] = jnp.where(first, whole[:half, :half], whole[half:, half:])
        out[pl.ds(half, half // 2), :] = jnp.where(first, whole[: half // 2, half:], whole[half // 2 : half, half:])


def first_kernel(flip, t, rows, a_ref, u_high, u_low, prods, *refs):
    out = refs[-1]
    col = lax.axis_index("col")
    group, h = col // rows, (col % 2) ^ flip
    nb, width = out.shape
    at = h * (lax.axis_size("col") // rows) + (group ^ t)
    value = product(split(prods[...]), (u_high[...], u_low[...]), NT)
    out[...] = tile_rows(a_ref, at * nb, nb, width, 0, width) - value


def last_kernel(places, rows, v_high, v_low, u_high, u_low, s_mine, s_other, *refs):
    *refs, out, inner, mixed, buf, sem = refs
    bases, prods = refs[: len(places)], refs[len(places) :]
    row, col = lax.axis_index("row"), lax.axis_index("col")
    core = row % 2
    half = inner.shape[0] // 2
    first = jnp.where(core == 0, s_mine[...], s_other[...])
    second = jnp.where(core == 0, s_other[...], s_mine[...])
    corner = jnp.concatenate([first[half:], second[half:]], axis=0)
    inner[:half, :half] = first[:half]
    inner[:half, half:] = corner
    inner[half:, :half] = corner.T
    inner[half:, half:] = second[:half]
    mixed[...] = product((u_high[...], u_low[...]), split(inner[...]), NT)
    count, ys = prods[0].shape[0], len(prods) // 2
    for k, ref in enumerate(prods):
        at = pl.ds(((core ^ k // ys) * ys + (row // 2 ^ k % ys)) * count, count)
        mixed[at, :] = mixed[at, :] - ref[...]
    right = split(mixed[...])
    nb, width = bases[0].shape
    step = width // LANES
    copies = []
    for k, (base, (flip, t)) in enumerate(zip(bases, places)):
        at = (col % 2 ^ flip) * (lax.axis_size("col") // rows) + (col // rows ^ t)
        rows_at = pl.ds(at * nb, nb)
        value = base[...] + product((v_high[rows_at, :], v_low[rows_at, :]), right, NT)
        for j in range(step):
            buf[k, pl.ds(j, nb, stride=step), :] = value[:, j * LANES : (j + 1) * LANES]
        copy = pltpu.make_async_copy(buf.at[k], out.at[pl.ds(at * nb * step, nb * step)], sem.at[k])
        copy.start()
        copies.append(copy)
    for copy in copies:
        copy.wait()


def per_device(matrix, vectors, t_factor):
    block_rows, _, nb, _ = vectors.shape
    width = matrix.shape[3] * nb
    rows, cols = lax.axis_size("row"), lax.axis_size("col")
    ratio, ys, zs = cols // rows, rows // 2, cols // 2
    row, col = lax.axis_index("row"), lax.axis_index("col")
    height, half, piece, share = block_rows * nb, width // 2, width // rows, nb // rows
    assert half == nb and block_rows == 2 * ratio
    step = width // LANES
    linear = matrix.reshape(height * step, LANES)
    vecs = vectors.reshape(height, nb)

    def move(value, target):
        return send(value, rows, cols, target)

    def other_core(r, c):
        return r ^ 1, c

    keep, give = call(
        functools.partial(sums_kernel, width),
        (sds(half, nb), sds(half, nb)),
        pltpu.with_memory_space_constraint(linear, pltpu.HBM),
        pltpu.with_memory_space_constraint(vecs, pltpu.HBM),
        specs=[HBM, HBM],
        scratch=[
            pltpu.VMEM((block_rows, nb * step, LANES), F32),
            pltpu.VMEM((block_rows, nb, nb), F32),
            pltpu.SemaphoreType.DMA((block_rows,)),
            pltpu.SemaphoreType.DMA((block_rows,)),
        ],
        limit=16,
    )
    piece = half // ys
    cuts = call(cut_kernel, [sds(piece, nb)] * ys, keep, move(give, other_core))

    def along_y(value):
        return [move(value, lambda r, c, s=s: (r ^ (2 * s), c)) for s in range(1, ys)]

    total = call(
        add_kernel,
        sds(piece, nb),
        cuts[0],
        *[move(cut, lambda r, c, s=s: (r ^ (2 * s), c)) for s, cut in enumerate(cuts) if s],
    )
    mine = [total, *along_y(total)]

    def target(r, c, t, s):
        group, twin = c // rows, c % rows // 2
        return twin * 2 + c % 2, (group ^ t) * rows + (r ^ (2 * s))

    straight = [
        call(
            join_kernel,
            sds(half, nb),
            *[move(total, lambda r, c, t=t, s=s: target(r, c, t, s)) for s in reversed(range(ys))][::-1],
        )
        for t in range(ratio)
    ]
    across = [move(value, lambda r, c: (r, c ^ 1)) for value in straight]

    own = call(functools.partial(own_kernel, rows), [sds(nb, nb)] * 2, keep, vecs, specs=[ANY, VMEM])
    came = move(own[1], lambda r, c: other_core(r, c) if r == c % rows else None)
    block = call(pick_core_kernel, sds(nb, nb), own[0], came)
    came = [
        move(block, lambda r, c, s=s: (r ^ (2 * s), c) if r // 2 == c % rows // 2 else None) for s in range(1, ys)
    ]
    near = call(pick_plane_kernel, sds(nb, nb), block, *came)
    u_high, u_low, v_high, v_low = call(
        scale_kernel,
        [sds(width, nb, dtype=BF16)] * 2 + [sds(height, nb, dtype=BF16)] * 2,
        vecs,
        near,
        move(near, other_core),
        t_factor,
    )
    other = [move(value, other_core) for value in mine]

    places = [(1, 1)] + [(0, t) for t in range(ratio)] + [(1, t) for t in range(ratio) if t != 1]
    bases = []
    for flip, t in places:
        bases.append(
            call(
                functools.partial(first_kernel, flip, t, rows),
                sds(nb, width),
                linear,
                u_high,
                u_low,
                (straight, across)[flip][t],
                *bases[-1:],
                specs=[VMEM] * 4 + [ANY] * len(bases[-1:]),
            )
        )
    keep, give = call(
        functools.partial(part_kernel, rows),
        (sds(3 * nb // 4, nb // 2), sds(3 * nb // 4, nb // 2)),
        vecs,
        *straight,
        scratch=[pltpu.VMEM((nb, nb), F32)],
    )
    share = late_add((), keep, move(give, other_core))
    share = late_add(bases[ratio : ratio + 1], share, *along_y(share))
    share = late_add(bases[-1:], share, move(share, lambda r, c: (r, c ^ 1)))
    rest = move(share, other_core)

    result = pl.pallas_call(
        functools.partial(last_kernel, places, rows),
        out_shape=sds(height * step, LANES),
        in_specs=[VMEM] * (6 + len(bases) + 2 * ys),
        out_specs=HBM,
        scratch_shapes=[
            pltpu.VMEM((nb, nb), F32),
            pltpu.VMEM((width, nb), F32),
            pltpu.VMEM((block_rows, nb * step, LANES), F32),
            pltpu.SemaphoreType.DMA((block_rows,)),
        ],
        compiler_params=pltpu.CompilerParams(vmem_limit_bytes=32 << 20),
    )(v_high, v_low, u_high, u_low, share, rest, *bases, *mine, *other)
    return result.reshape(matrix.shape)


def solution(mesh):
    in_specs = (P(None, "row", None, None, "col", None), P(None, "row", None, None), P())
    out_specs = P(None, "row", None, None, "col", None)
    return jax.shard_map(
        per_device, mesh=mesh, in_specs=in_specs, out_specs=out_specs, check_vma=False
    )
```

```python
import functools

import jax
import jax.numpy as jnp
from jax import lax
from jax.experimental import pallas as pl
from jax.experimental.pallas import tpu as pltpu
from jax.sharding import PartitionSpec as P

AXES = ("row", "col")
F32, BF16 = jnp.float32, jnp.bfloat16
NN, NT, TN = ((1,), (0,)), ((1,), (1,)), ((0,), (0,))
LANES = 128
VMEM = pl.BlockSpec(memory_space=pltpu.VMEM)
HBM = pl.BlockSpec(memory_space=pltpu.HBM)
ANY = pl.BlockSpec(memory_space=pl.ANY)


def split(value):
    high = value.astype(BF16)
    return high, (value - high.astype(F32)).astype(BF16)


def product(left, right, dims):
    def one(a, b):
        return lax.dot_general(a, b, (dims, ((), ())), preferred_element_type=F32)

    (lh, ll), (rh, rl) = left, right
    return one(lh, rh) + (one(lh, rl) + one(ll, rh))


def sds(*shape, dtype=F32):
    return jax.ShapeDtypeStruct(shape, dtype)


def call(kernel, outs, *args, specs=None, scratch=(), limit=32):
    return pl.pallas_call(
        kernel,
        out_shape=outs,
        in_specs=specs or [VMEM] * len(args),
        out_specs=jax.tree.map(lambda _: VMEM, outs),
        scratch_shapes=list(scratch),
        compiler_params=pltpu.CompilerParams(vmem_limit_bytes=limit << 20),
    )(*args)


def send(value, rows, cols, target):
    pairs = []
    for row in range(rows):
        for col in range(cols):
            to = target(row, col)
            if to is not None:
                pairs.append((row * cols + col, to[0] * cols + to[1]))
    return lax.ppermute(value, AXES, pairs)


def with_unit_top(block):
    size = block.shape[0]
    i = lax.broadcasted_iota(jnp.int32, (size, size), 0)
    j = lax.broadcasted_iota(jnp.int32, (size, size), 1)
    unit = jnp.where(i > j, block, jnp.where(i == j, 1.0, 0.0))
    return jnp.where(lax.axis_index("row") == 0, unit, block)


def tile_rows(ref, start, count, width, first, lanes):
    step = width // LANES
    return jnp.concatenate(
        [ref[pl.ds(start * step + first + k, count, stride=step), :] for k in range(lanes // LANES)], axis=1
    )


def sums_kernel(width, a_hbm, v_hbm, keep, give, a_buf, v_buf, a_sem, v_sem):
    nb = v_buf.shape[1]
    count, step = v_buf.shape[0], width // LANES
    core = lax.axis_index("row") % 2
    copies = []
    for b in range(count):
        v_copy = pltpu.make_async_copy(v_hbm.at[pl.ds(b * nb, nb)], v_buf.at[b], v_sem.at[b])
        a_copy = pltpu.make_async_copy(a_hbm.at[pl.ds(b * nb * step, nb * step)], a_buf.at[b], a_sem.at[b])
        v_copy.start()
        a_copy.start()
        copies.append((v_copy, a_copy))
    for b in range(count):
        copies[b][0].wait()
        block = v_buf[b]
        if b == 0:
            block = with_unit_top(block)
        right = split(block)
        copies[b][1].wait()
        for out, half in ((give, 1 - core), (keep, core)):
            left = split(tile_rows(a_buf.at[b], 0, nb, width, half * (nb // LANES), nb))
            value = product(left, right, TN)
            out[...] = value if b == 0 else out[...] + value


def add_kernel(*refs):
    *terms, out = refs
    total = terms[0][...]
    for term in terms[1:]:
        total = total + term[...]
    out[...] = total


def cut_kernel(keep, came, *parts):
    y, count = lax.axis_index("row") // 2, parts[0].shape[0]
    for s, part in enumerate(parts):
        at = pl.ds((y ^ s) * count, count)
        part[...] = keep[at, :] + came[at, :]


def join_kernel(*refs):
    *pieces, out = refs
    count = pieces[0].shape[0]
    y = lax.axis_index("col") % lax.axis_size("row") // 2
    for s, piece in enumerate(pieces):
        out[pl.ds((y ^ s) * count, count), :] = piece[...]


def late_add_kernel(count, *refs):
    add_kernel(*refs[count:])


def late_add(ready, *terms):
    return call(
        functools.partial(late_add_kernel, len(ready)),
        sds(*terms[0].shape),
        *ready,
        *terms,
        specs=[ANY] * len(ready) + [VMEM] * len(terms),
    )


def own_kernel(rows, _, v_ref, *outs):
    nb = v_ref.shape[1]
    group, ratio = lax.axis_index("col") // rows, lax.axis_size("col") // rows
    core = lax.axis_index("row") % 2
    for k, out in zip((core, 1 - core), outs):
        at = k * ratio + group
        block = v_ref[pl.ds(at * nb, nb), :]
        out[...] = jnp.where(at == 0, with_unit_top(block), block)


def pick_core_kernel(mine, came, out):
    same = lax.axis_index("row") % 2 == lax.axis_index("col") % 2
    out[...] = jnp.where(same, mine[...], came[...])


def pick_plane_kernel(mine, *refs):
    *vecs, out = refs
    rows = lax.axis_size("row")
    same = lax.axis_index("row") // 2 == lax.axis_index("col") % rows // 2
    came = vecs[0][...]
    for ref in vecs[1:]:
        came = came + ref[...]
    out[...] = jnp.where(same, mine[...], came)


def scale_kernel(v_ref, mine, other, t_ref, high, low, v_high, v_low):
    nb = mine.shape[0]
    core = lax.axis_index("row") % 2
    right = split(t_ref[...])
    for k, ref in zip((core, 1 - core), (mine, other)):
        at = pl.ds(k * nb, nb)
        high[at, :], low[at, :] = split(product(split(ref[...]), right, NT))
    for b in range(v_ref.shape[0] // nb):
        at = pl.ds(b * nb, nb)
        block = v_ref[at, :]
        if b == 0:
            block = with_unit_top(block)
        v_high[at, :], v_low[at, :] = split(product(split(block), right, NT))


def part_kernel(rows, v_ref, *refs):
    *arrays, keep, give, whole = refs
    nb, half = whole.shape[0], whole.shape[0] // 2
    col, core = lax.axis_index("col"), lax.axis_index("row") % 2
    group, x = col // rows, col % 2
    value = 0.0
    for t, array in enumerate(arrays):
        at = x * len(arrays) + (group ^ t)
        block = v_ref[pl.ds(at * nb, nb), :]
        block = jnp.where(at == 0, with_unit_top(block), block)
        value = value + product(split(block), split(array[...]), TN)
    whole[...] = value
    part = half // 2
    for out, first in ((keep, core == 0), (give, core == 1)):
        diagonal = jnp.where(first, whole[:half, :half], whole[half:, half:])
        last = diagonal[part:, part:]
        out[:part] = diagonal[:part]
        out[part : part + part // 2] = jnp.concatenate([last[: part // 2], last[part // 2 :]], axis=1)
        out[part + part // 2 :] = jnp.where(first, whole[:part, half:], whole[part:half, half:])


def first_kernel(flip, t, rows, a_ref, u_high, u_low, prods, *refs):
    out = refs[-1]
    col = lax.axis_index("col")
    group, h = col // rows, (col % 2) ^ flip
    nb, width = out.shape
    at = h * (lax.axis_size("col") // rows) + (group ^ t)
    value = product(split(prods[...]), (u_high[...], u_low[...]), NT)
    out[...] = tile_rows(a_ref, at * nb, nb, width, 0, width) - value


def last_kernel(places, rows, v_high, v_low, u_high, u_low, s_mine, s_other, *refs):
    *refs, out, inner, mixed, buf, sem = refs
    bases, prods = refs[: len(places)], refs[len(places) :]
    row, col = lax.axis_index("row"), lax.axis_index("col")
    core = row % 2
    half = inner.shape[0] // 2
    first = jnp.where(core == 0, s_mine[...], s_other[...])
    second = jnp.where(core == 0, s_other[...], s_mine[...])
    part = half // 2
    split_at = part + part // 2
    corner = jnp.concatenate([first[split_at:], second[split_at:]], axis=0)
    for k, share in enumerate((first, second)):
        last = share[part:split_at]
        last = jnp.concatenate([last[:, :part], last[:, part:]], axis=0)
        lower = jnp.concatenate([share[:part, part:].T, last], axis=1)
        at = pl.ds(k * half, half)
        inner[at, at] = jnp.concatenate([share[:part], lower], axis=0)
    inner[:half, half:] = corner
    inner[half:, :half] = corner.T
    mixed[...] = product((u_high[...], u_low[...]), split(inner[...]), NT)
    count, ys = prods[0].shape[0], len(prods) // 2
    for k, ref in enumerate(prods):
        at = pl.ds(((core ^ k // ys) * ys + (row // 2 ^ k % ys)) * count, count)
        mixed[at, :] = mixed[at, :] - ref[...]
    right = split(mixed[...])
    nb, width = bases[0].shape
    step = width // LANES
    copies = []
    for k, (base, (flip, t)) in enumerate(zip(bases, places)):
        at = (col % 2 ^ flip) * (lax.axis_size("col") // rows) + (col // rows ^ t)
        rows_at = pl.ds(at * nb, nb)
        value = base[...] + product((v_high[rows_at, :], v_low[rows_at, :]), right, NT)
        for j in range(step):
            buf[k, pl.ds(j, nb, stride=step), :] = value[:, j * LANES : (j + 1) * LANES]
        copy = pltpu.make_async_copy(buf.at[k], out.at[pl.ds(at * nb * step, nb * step)], sem.at[k])
        copy.start()
        copies.append(copy)
    for copy in copies:
        copy.wait()


def per_device(matrix, vectors, t_factor):
    block_rows, _, nb, _ = vectors.shape
    width = matrix.shape[3] * nb
    rows, cols = lax.axis_size("row"), lax.axis_size("col")
    ratio, ys, zs = cols // rows, rows // 2, cols // 2
    row, col = lax.axis_index("row"), lax.axis_index("col")
    height, half, piece, share = block_rows * nb, width // 2, width // rows, nb // rows
    assert half == nb and block_rows == 2 * ratio
    step = width // LANES
    linear = matrix.reshape(height * step, LANES)
    vecs = vectors.reshape(height, nb)

    def move(value, target):
        return send(value, rows, cols, target)

    def other_core(r, c):
        return r ^ 1, c

    keep, give = call(
        functools.partial(sums_kernel, width),
        (sds(half, nb), sds(half, nb)),
        pltpu.with_memory_space_constraint(linear, pltpu.HBM),
        pltpu.with_memory_space_constraint(vecs, pltpu.HBM),
        specs=[HBM, HBM],
        scratch=[
            pltpu.VMEM((block_rows, nb * step, LANES), F32),
            pltpu.VMEM((block_rows, nb, nb), F32),
            pltpu.SemaphoreType.DMA((block_rows,)),
            pltpu.SemaphoreType.DMA((block_rows,)),
        ],
        limit=16,
    )
    piece = half // ys
    cuts = call(cut_kernel, [sds(piece, nb)] * ys, keep, move(give, other_core))

    def along_y(value):
        return [move(value, lambda r, c, s=s: (r ^ (2 * s), c)) for s in range(1, ys)]

    total = call(
        add_kernel,
        sds(piece, nb),
        cuts[0],
        *[move(cut, lambda r, c, s=s: (r ^ (2 * s), c)) for s, cut in enumerate(cuts) if s],
    )
    mine = [total, *along_y(total)]

    def target(r, c, t, s):
        group, twin = c // rows, c % rows // 2
        return twin * 2 + c % 2, (group ^ t) * rows + (r ^ (2 * s))

    straight = [
        call(
            join_kernel,
            sds(half, nb),
            *[move(total, lambda r, c, t=t, s=s: target(r, c, t, s)) for s in reversed(range(ys))][::-1],
        )
        for t in range(ratio)
    ]
    across = [move(value, lambda r, c: (r, c ^ 1)) for value in straight]

    own = call(functools.partial(own_kernel, rows), [sds(nb, nb)] * 2, keep, vecs, specs=[ANY, VMEM])
    came = move(own[1], lambda r, c: other_core(r, c) if r == c % rows else None)
    block = call(pick_core_kernel, sds(nb, nb), own[0], came)
    came = [
        move(block, lambda r, c, s=s: (r ^ (2 * s), c) if r // 2 == c % rows // 2 else None) for s in range(1, ys)
    ]
    near = call(pick_plane_kernel, sds(nb, nb), block, *came)
    u_high, u_low, v_high, v_low = call(
        scale_kernel,
        [sds(width, nb, dtype=BF16)] * 2 + [sds(height, nb, dtype=BF16)] * 2,
        vecs,
        near,
        move(near, other_core),
        t_factor,
    )
    other = [move(value, other_core) for value in mine]

    places = [(1, 1)] + [(0, t) for t in range(ratio)] + [(1, t) for t in range(ratio) if t != 1]
    bases = []
    for flip, t in places:
        bases.append(
            call(
                functools.partial(first_kernel, flip, t, rows),
                sds(nb, width),
                linear,
                u_high,
                u_low,
                (straight, across)[flip][t],
                *bases[-1:],
                specs=[VMEM] * 4 + [ANY] * len(bases[-1:]),
            )
        )
    keep, give = call(
        functools.partial(part_kernel, rows),
        (sds(5 * nb // 8, nb // 2), sds(5 * nb // 8, nb // 2)),
        vecs,
        *straight,
        scratch=[pltpu.VMEM((nb, nb), F32)],
    )
    share = late_add((), keep, move(give, other_core))
    share = late_add(bases[ratio : ratio + 1], share, *along_y(share))
    share = late_add(bases[-1:], share, move(share, lambda r, c: (r, c ^ 1)))
    rest = move(share, other_core)

    result = pl.pallas_call(
        functools.partial(last_kernel, places, rows),
        out_shape=sds(height * step, LANES),
        in_specs=[VMEM] * (6 + len(bases) + 2 * ys),
        out_specs=HBM,
        scratch_shapes=[
            pltpu.VMEM((nb, nb), F32),
            pltpu.VMEM((width, nb), F32),
            pltpu.VMEM((block_rows, nb * step, LANES), F32),
            pltpu.SemaphoreType.DMA((block_rows,)),
        ],
        compiler_params=pltpu.CompilerParams(vmem_limit_bytes=32 << 20),
    )(v_high, v_low, u_high, u_low, share, rest, *bases, *mine, *other)
    return result.reshape(matrix.shape)


def solution(mesh):
    in_specs = (P(None, "row", None, None, "col", None), P(None, "row", None, None), P())
    out_specs = P(None, "row", None, None, "col", None)
    return jax.shard_map(
        per_device, mesh=mesh, in_specs=in_specs, out_specs=out_specs, check_vma=False
    )
```

```python
import functools

import jax
import jax.numpy as jnp
from jax import lax
from jax.experimental import pallas as pl
from jax.experimental.pallas import tpu as pltpu
from jax.sharding import PartitionSpec as P

AXES = ("row", "col")
F32, BF16 = jnp.float32, jnp.bfloat16
NN, NT, TN = ((1,), (0,)), ((1,), (1,)), ((0,), (0,))
LANES = 128
VMEM = pl.BlockSpec(memory_space=pltpu.VMEM)
HBM = pl.BlockSpec(memory_space=pltpu.HBM)
ANY = pl.BlockSpec(memory_space=pl.ANY)


def split(value):
    high = value.astype(BF16)
    return high, (value - high.astype(F32)).astype(BF16)


def product(left, right, dims):
    def one(a, b):
        return lax.dot_general(a, b, (dims, ((), ())), preferred_element_type=F32)

    (lh, ll), (rh, rl) = left, right
    return one(lh, rh) + (one(lh, rl) + one(ll, rh))


def sds(*shape, dtype=F32):
    return jax.ShapeDtypeStruct(shape, dtype)


def call(kernel, outs, *args, specs=None, scratch=(), limit=32):
    return pl.pallas_call(
        kernel,
        out_shape=outs,
        in_specs=specs or [VMEM] * len(args),
        out_specs=jax.tree.map(lambda _: VMEM, outs),
        scratch_shapes=list(scratch),
        compiler_params=pltpu.CompilerParams(vmem_limit_bytes=limit << 20),
    )(*args)


def send(value, rows, cols, target):
    pairs = []
    for row in range(rows):
        for col in range(cols):
            to = target(row, col)
            if to is not None:
                pairs.append((row * cols + col, to[0] * cols + to[1]))
    return lax.ppermute(value, AXES, pairs)


def with_unit_top(block):
    size = block.shape[0]
    i = lax.broadcasted_iota(jnp.int32, (size, size), 0)
    j = lax.broadcasted_iota(jnp.int32, (size, size), 1)
    unit = jnp.where(i > j, block, jnp.where(i == j, 1.0, 0.0))
    return jnp.where(lax.axis_index("row") == 0, unit, block)


def tile_rows(ref, start, count, width, first, lanes):
    step = width // LANES
    return jnp.concatenate(
        [ref[pl.ds(start * step + first + k, count, stride=step), :] for k in range(lanes // LANES)], axis=1
    )


def sums_kernel(width, a_hbm, v_hbm, keep, give, a_buf, v_buf, a_sem, v_sem):
    nb = v_buf.shape[1]
    count, step = v_buf.shape[0], width // LANES
    core = lax.axis_index("row") % 2
    copies = []
    for b in range(count):
        v_copy = pltpu.make_async_copy(v_hbm.at[pl.ds(b * nb, nb)], v_buf.at[b], v_sem.at[b])
        a_copy = pltpu.make_async_copy(a_hbm.at[pl.ds(b * nb * step, nb * step)], a_buf.at[b], a_sem.at[b])
        v_copy.start()
        a_copy.start()
        copies.append((v_copy, a_copy))
    for b in range(count):
        copies[b][0].wait()
        block = v_buf[b]
        if b == 0:
            block = with_unit_top(block)
        right = split(block)
        copies[b][1].wait()
        for out, half in ((give, 1 - core), (keep, core)):
            left = split(tile_rows(a_buf.at[b], 0, nb, width, half * (nb // LANES), nb))
            value = product(left, right, TN)
            out[...] = value if b == 0 else out[...] + value


def add_kernel(*refs):
    *terms, out = refs
    total = terms[0][...]
    for term in terms[1:]:
        total = total + term[...]
    out[...] = total


def cut_kernel(keep, came, *parts):
    y, count = lax.axis_index("row") // 2, parts[0].shape[0]
    for s, part in enumerate(parts):
        at = pl.ds((y ^ s) * count, count)
        part[...] = keep[at, :] + came[at, :]


def join_kernel(*refs):
    *pieces, out = refs
    count = pieces[0].shape[0]
    y = lax.axis_index("col") % lax.axis_size("row") // 2
    for s, piece in enumerate(pieces):
        out[pl.ds((y ^ s) * count, count), :] = piece[...]


def late_add_kernel(count, *refs):
    add_kernel(*refs[count:])


def late_add(ready, *terms):
    return call(
        functools.partial(late_add_kernel, len(ready)),
        sds(*terms[0].shape),
        *ready,
        *terms,
        specs=[ANY] * len(ready) + [VMEM] * len(terms),
    )


def own_kernel(rows, _, v_ref, *outs):
    nb = v_ref.shape[1]
    group, ratio = lax.axis_index("col") // rows, lax.axis_size("col") // rows
    core = lax.axis_index("row") % 2
    for k, out in zip((core, 1 - core), outs):
        at = k * ratio + group
        block = v_ref[pl.ds(at * nb, nb), :]
        out[...] = jnp.where(at == 0, with_unit_top(block), block)


def pick_core_kernel(mine, came, out):
    same = lax.axis_index("row") % 2 == lax.axis_index("col") % 2
    out[...] = jnp.where(same, mine[...], came[...])


def pick_plane_kernel(mine, *refs):
    *vecs, out = refs
    rows = lax.axis_size("row")
    same = lax.axis_index("row") // 2 == lax.axis_index("col") % rows // 2
    came = vecs[0][...]
    for ref in vecs[1:]:
        came = came + ref[...]
    out[...] = jnp.where(same, mine[...], came)


def scale_kernel(v_ref, mine, other, t_ref, high, low, v_high, v_low):
    nb = mine.shape[0]
    core = lax.axis_index("row") % 2
    right = split(t_ref[...])
    for k, ref in zip((core, 1 - core), (mine, other)):
        at = pl.ds(k * nb, nb)
        high[at, :], low[at, :] = split(product(split(ref[...]), right, NT))
    for b in range(v_ref.shape[0] // nb):
        at = pl.ds(b * nb, nb)
        block = v_ref[at, :]
        if b == 0:
            block = with_unit_top(block)
        v_high[at, :], v_low[at, :] = split(product(split(block), right, NT))


def part_kernel(rows, v_ref, *refs):
    *arrays, keep, give, whole = refs
    nb, half = whole.shape[0], whole.shape[0] // 2
    col, core = lax.axis_index("col"), lax.axis_index("row") % 2
    group, x = col // rows, col % 2
    value = 0.0
    for t, array in enumerate(arrays):
        at = x * len(arrays) + (group ^ t)
        block = v_ref[pl.ds(at * nb, nb), :]
        block = jnp.where(at == 0, with_unit_top(block), block)
        value = value + product(split(block), split(array[...]), TN)
    whole[...] = value
    part = half // 2
    for out, first in ((keep, core == 0), (give, core == 1)):
        diagonal = jnp.where(first, whole[:half, :half], whole[half:, half:])
        last = diagonal[part:, part:]
        out[:part] = diagonal[:part]
        out[part : part + part // 2] = jnp.concatenate([last[: part // 2], last[part // 2 :]], axis=1)
        out[part + part // 2 :] = jnp.where(first, whole[:part, half:], whole[part:half, half:])


def first_kernel(flip, t, rows, a_ref, u_high, u_low, prods, *refs):
    out = refs[-1]
    col = lax.axis_index("col")
    group, h = col // rows, (col % 2) ^ flip
    nb, width = out.shape
    at = h * (lax.axis_size("col") // rows) + (group ^ t)
    value = product(split(prods[...]), (u_high[...], u_low[...]), NT)
    out[...] = tile_rows(a_ref, at * nb, nb, width, 0, width) - value


def last_kernel(places, rows, v_high, v_low, u_high, u_low, s_mine, s_other, *refs):
    *refs, out, inner, mixed, buf, sem = refs
    bases, prods = refs[: len(places)], refs[len(places) :]
    row, col = lax.axis_index("row"), lax.axis_index("col")
    core = row % 2
    half = inner.shape[0] // 2
    first = jnp.where(core == 0, s_mine[...], s_other[...])
    second = jnp.where(core == 0, s_other[...], s_mine[...])
    part = half // 2
    split_at = part + part // 2
    corner = jnp.concatenate([first[split_at:], second[split_at:]], axis=0)
    for k, share in enumerate((first, second)):
        last = share[part:split_at]
        last = jnp.concatenate([last[:, :part], last[:, part:]], axis=0)
        lower = jnp.concatenate([share[:part, part:].T, last], axis=1)
        at = pl.ds(k * half, half)
        inner[at, at] = jnp.concatenate([share[:part], lower], axis=0)
    inner[:half, half:] = corner
    inner[half:, :half] = corner.T
    mixed[...] = product((u_high[...], u_low[...]), split(inner[...]), NT)
    count, ys = prods[0].shape[0], len(prods) // 2
    for k, ref in enumerate(prods):
        at = pl.ds(((core ^ k // ys) * ys + (row // 2 ^ k % ys)) * count, count)
        mixed[at, :] = mixed[at, :] - ref[...]
    right = split(mixed[...])
    nb, width = bases[0].shape
    step = width // LANES
    copies = []
    for k, (base, (flip, t)) in enumerate(zip(bases, places)):
        at = (col % 2 ^ flip) * (lax.axis_size("col") // rows) + (col // rows ^ t)
        rows_at = pl.ds(at * nb, nb)
        value = base[...] + product((v_high[rows_at, :], v_low[rows_at, :]), right, NT)
        for j in range(step):
            buf[k, pl.ds(j, nb, stride=step), :] = value[:, j * LANES : (j + 1) * LANES]
        copy = pltpu.make_async_copy(buf.at[k], out.at[pl.ds(at * nb * step, nb * step)], sem.at[k])
        copy.start()
        copies.append(copy)
    for copy in copies:
        copy.wait()


def per_device(matrix, vectors, t_factor):
    block_rows, _, nb, _ = vectors.shape
    width = matrix.shape[3] * nb
    rows, cols = lax.axis_size("row"), lax.axis_size("col")
    ratio, ys, zs = cols // rows, rows // 2, cols // 2
    row, col = lax.axis_index("row"), lax.axis_index("col")
    height, half, piece, share = block_rows * nb, width // 2, width // rows, nb // rows
    assert half == nb and block_rows == 2 * ratio
    step = width // LANES
    linear = matrix.reshape(height * step, LANES)
    vecs = vectors.reshape(height, nb)

    def move(value, target):
        return send(value, rows, cols, target)

    def other_core(r, c):
        return r ^ 1, c

    keep, give = call(
        functools.partial(sums_kernel, width),
        (sds(half, nb), sds(half, nb)),
        pltpu.with_memory_space_constraint(linear, pltpu.HBM),
        pltpu.with_memory_space_constraint(vecs, pltpu.HBM),
        specs=[HBM, HBM],
        scratch=[
            pltpu.VMEM((block_rows, nb * step, LANES), F32),
            pltpu.VMEM((block_rows, nb, nb), F32),
            pltpu.SemaphoreType.DMA((block_rows,)),
            pltpu.SemaphoreType.DMA((block_rows,)),
        ],
        limit=16,
    )
    piece = half // ys
    cuts = call(cut_kernel, [sds(piece, nb)] * ys, keep, move(give, other_core))

    def along_y(value):
        return [move(value, lambda r, c, s=s: (r ^ (2 * s), c)) for s in range(1, ys)]

    total = call(
        add_kernel,
        sds(piece, nb),
        cuts[0],
        *[move(cut, lambda r, c, s=s: (r ^ (2 * s), c)) for s, cut in enumerate(cuts) if s],
    )
    mine = [total, *along_y(total)]

    def target(r, c, t, s):
        group, twin = c // rows, c % rows // 2
        return twin * 2 + c % 2, (group ^ t) * rows + (r ^ (2 * s))

    straight = [
        call(
            join_kernel,
            sds(half, nb),
            *[move(total, lambda r, c, t=t, s=s: target(r, c, t, s)) for s in reversed(range(ys))][::-1],
        )
        for t in range(ratio)
    ]
    across = [move(value, lambda r, c: (r, c ^ 1)) for value in straight]

    own = call(functools.partial(own_kernel, rows), [sds(nb, nb)] * 2, keep, vecs, specs=[ANY, VMEM])
    came = move(own[1], lambda r, c: other_core(r, c) if r == c % rows else None)
    block = call(pick_core_kernel, sds(nb, nb), own[0], came)
    came = [
        move(block, lambda r, c, s=s: (r ^ (2 * s), c) if r // 2 == c % rows // 2 else None) for s in range(1, ys)
    ]
    near = call(pick_plane_kernel, sds(nb, nb), block, *came)
    u_high, u_low, v_high, v_low = call(
        scale_kernel,
        [sds(width, nb, dtype=BF16)] * 2 + [sds(height, nb, dtype=BF16)] * 2,
        vecs,
        near,
        move(near, other_core),
        t_factor,
    )
    other = [move(value, other_core) for value in mine]

    places = [(1, 1)] + [(0, t) for t in range(ratio)] + [(1, t) for t in range(ratio) if t != 1]
    bases = []
    for flip, t in places:
        bases.append(
            call(
                functools.partial(first_kernel, flip, t, rows),
                sds(nb, width),
                linear,
                u_high,
                u_low,
                (straight, across)[flip][t],
                *bases[-1:],
                specs=[VMEM] * 4 + [ANY] * len(bases[-1:]),
            )
        )
    keep, give = call(
        functools.partial(part_kernel, rows),
        (sds(5 * nb // 8, nb // 2), sds(5 * nb // 8, nb // 2)),
        vecs,
        *straight,
        scratch=[pltpu.VMEM((nb, nb), F32)],
    )
    share = late_add((), keep, move(give, other_core))
    share = late_add(bases[:1], share, *along_y(share))
    share = late_add(bases[-1:], share, move(share, lambda r, c: (r, c ^ 1)))
    rest = move(share, other_core)

    result = pl.pallas_call(
        functools.partial(last_kernel, places, rows),
        out_shape=sds(height * step, LANES),
        in_specs=[VMEM] * (6 + len(bases) + 2 * ys),
        out_specs=HBM,
        scratch_shapes=[
            pltpu.VMEM((nb, nb), F32),
            pltpu.VMEM((width, nb), F32),
            pltpu.VMEM((block_rows, nb * step, LANES), F32),
            pltpu.SemaphoreType.DMA((block_rows,)),
        ],
        compiler_params=pltpu.CompilerParams(vmem_limit_bytes=32 << 20),
    )(v_high, v_low, u_high, u_low, share, rest, *bases, *mine, *other)
    return result.reshape(matrix.shape)


def solution(mesh):
    in_specs = (P(None, "row", None, None, "col", None), P(None, "row", None, None), P())
    out_specs = P(None, "row", None, None, "col", None)
    return jax.shard_map(
        per_device, mesh=mesh, in_specs=in_specs, out_specs=out_specs, check_vma=False
    )
```
